256 devices in a mesh: sign: 2 (over y_hi), context: 128 (over y_lo, x, z, core).
Axes of the slice: x: 4, y: 4 (y_hi: 2, y_lo: 2; y = y_hi * 2 + y_lo), z: 8, core: 2. Of those that a mesh axis runs over, the one named last changes fastest.
Arguments:
- inputs: bfloat16 [32768, 1024], P('context'), may hold values from -6 to 6
- cotangent: bfloat16 [32768, 1024], P('context'), may hold values from -24 to 24
- weights: bfloat16 [2, 1024, 1024], P('sign'), may hold values from -0.1875 to 0.1875
- filter_taps: float32 [32768], replicated, may hold values from -0.03125 to 0.03125
Outputs:
- input_grad: bfloat16 [32768, 1024], P('context', 'sign')
- weight_grad: float32 [2, 1024, 1024], P('sign', 'context')
The draws below stay inside these ranges and needn't reach their ends.
All inputs are finite; a program needn't handle non-finite values.
Results may differ from the reference program's by a relative error of at most 0.0058.
Values may be sent and summed in bfloat16 or wider, within the bound.
No kernel may reach another device: no remote copies, remote signals or barrier semaphores. Data moves between devices by JAX's collectives and lax.ppermute only.
A program may use at most 64 MiB of HBM per device.

```python
import math
import jax
import jax.numpy as jnp

D = 1024
TOKENS = 32768


def raised(drawn, own_key, source, target, blocks, factor):
    owner, partner = [(jnp.arange(drawn.shape[position]) // (drawn.shape[position] // blocks)).reshape([-1 if axis == position else 1 for axis in range(drawn.ndim)]) for position in (source, target)]
    chosen = jax.random.permutation(own_key, blocks)[partner]
    strong = (owner == chosen) | (owner == (partner + blocks // 2) % blocks)
    return jnp.where(strong, factor * drawn, drawn)


def shard_levels(key, dims, cuts, low, high):
    factor_of = 1.0
    for position, shards_of in cuts:
        draws = jax.random.uniform(jax.random.fold_in(jax.random.fold_in(key, 6), position), (shards_of,), jnp.float32, low / len(cuts), high / len(cuts))
        factor_of = factor_of * jnp.repeat(jnp.exp(draws), dims[position] // shards_of).reshape((-1,) + (1,) * (len(dims) - 1 - position))
    return factor_of


def centred(own_key, extent, deviation, limit, shards=(), dtype=jnp.bfloat16):
    drawn = jax.random.normal(own_key, extent, jnp.float32) * deviation
    if len(shards) > 0:
        drawn = shard_levels(own_key, extent, shards, -0.22, 0.18) * drawn
    return jnp.clip(drawn, min=-limit, max=limit).astype(dtype)


def noise_with(key, dims, scale, most, shards, heavy, held_as=jnp.bfloat16):
    array = scale * jax.random.normal(key, dims, jnp.float32)
    if shards:
        array = array * shard_levels(key, dims, shards, -0.22, 0.18)
    return jnp.clip(raised(array, jax.random.fold_in(key, 3), *heavy), -most, most).astype(held_as)


def setup_inputs(seed: int = 0) -> dict:
    keys = jax.random.split(jax.random.key(seed), 5)
    inputs = centred(keys[0], (TOKENS, D), 1.0, 6.0, ((0, 128),))
    cotangent = noise_with(keys[1], (TOKENS, D), 1.0, 24.0, ((0, 128),), (0, 1, 128, 5.5))
    weights = centred(keys[2], (2, D, D), D ** -0.5, 0.1875, ((0, 2),))
    filter_taps = centred(keys[3], (TOKENS,), TOKENS ** -0.5, 0.03125, (), jnp.float32)
    return {"inputs": inputs, "cotangent": cotangent, "weights": weights, "filter_taps": filter_taps}


def filtered(signal, kernel, adjoint):
    padded_len = 2 * TOKENS
    signal_spec = jnp.fft.rfft(signal, n=padded_len, axis=0)
    kernel_spec = jnp.fft.rfft(kernel, n=padded_len)
    if adjoint:
        kernel_spec = jnp.conj(kernel_spec)
    return jnp.fft.irfft(signal_spec * kernel_spec[:, None], n=padded_len, axis=0)[:TOKENS]

def reference(inputs, cotangent, weights, filter_taps):
    lag_index = jnp.arange(TOKENS)
    alternate = jnp.where(lag_index % 2 == 0, filter_taps, -filter_taps)
    grad_scale = 1.0 / math.sqrt(TOKENS)
    summed = jnp.zeros((TOKENS, D), jnp.float32)
    weight_grads = []
    for signed in range(2):
        kernel = filter_taps if signed == 0 else alternate
        features = filtered(inputs.astype(jnp.float32), kernel, False).astype(jnp.bfloat16)
        weight_grads.append(jnp.dot(cotangent.T, features, preferred_element_type=jnp.float32) * grad_scale)
        feature_grad = jnp.dot(cotangent, weights[signed], preferred_element_type=jnp.float32).astype(jnp.bfloat16)
        backward = filtered(feature_grad.astype(jnp.float32), kernel, True).astype(jnp.bfloat16)
        summed = summed + backward.astype(jnp.float32)
    return (summed.astype(jnp.bfloat16), jnp.stack(weight_grads))
```

```python
import math

import jax
import jax.numpy as jnp
from jax import lax
from jax.experimental import pallas as pl
from jax.experimental.pallas import tpu as pltpu
from jax.sharding import Mesh, PartitionSpec as P

BF16, F32 = jnp.bfloat16, jnp.float32
LANES = 128
AXES = ("s", "yl", "x", "z", "c")
SIZES = (2, 2, 4, 8, 2)
VMEM = pl.BlockSpec(memory_space=pltpu.VMEM)


def toeplitz_kernel(taps_ref, out_ref, rows):
    blocks = out_ref.shape[0] // LANES
    source = lax.broadcasted_iota(jnp.int32, (2 * LANES, 2 * LANES), 0)
    target = lax.broadcasted_iota(jnp.int32, (2 * LANES, 2 * LANES), 1)
    select = source == 2 * (LANES - 1 - target % LANES) + target // LANES

    @pl.when(pl.program_id(0) == 0)
    def _():
        chosen = jnp.dot(
            taps_ref[...],
            select.astype(F32),
            precision=lax.Precision.HIGHEST,
            preferred_element_type=F32,
        )
        for parity in range(2):
            rows[parity, 0:8, :] = jnp.zeros((8, LANES), F32)
            rows[parity, 8:, :] = chosen[:, parity * LANES : (parity + 1) * LANES]

    keep = lax.broadcasted_iota(jnp.int32, (LANES, LANES), 1) < LANES - 1 - lax.broadcasted_iota(
        jnp.int32, (LANES, LANES), 0
    )
    first = pl.program_id(0) * blocks

    def body(m, carry):
        row = pl.multiple_of(m * LANES, LANES)
        for parity in range(2):
            before = jnp.broadcast_to(rows[parity, pl.ds(first + m + 7, 1), :], (LANES, LANES))
            here = jnp.broadcast_to(rows[parity, pl.ds(first + m + 8, 1), :], (LANES, LANES))
            tile = pltpu.roll(jnp.where(keep, before, here), 1, 1, stride=1, stride_axis=0)
            high = tile.astype(BF16)
            out_ref[pl.ds(row, LANES), parity * LANES : (parity + 1) * LANES] = high
            out_ref[pl.ds(row, LANES), (2 + parity) * LANES : (3 + parity) * LANES] = (
                tile - high.astype(F32)
            ).astype(BF16)
        return carry

    lax.fori_loop(0, blocks, body, 0, unroll=4)


def toeplitz(filter_taps):
    count = filter_taps.shape[0] // 2
    parts = 8
    return pl.pallas_call(
        toeplitz_kernel,
        grid=(parts,),
        out_shape=pltpu.MemorySpace.HBM((count, 4 * LANES), BF16),
        in_specs=[pl.BlockSpec((count // LANES, 2 * LANES), lambda i: (0, 0))],
        out_specs=pl.BlockSpec((count // parts, 4 * LANES), lambda i: (i, 0)),
        scratch_shapes=[pltpu.VMEM((2, count // LANES + 8, LANES), F32)],
        compiler_params=pltpu.CompilerParams(vmem_limit_bytes=16 << 20),
        cost_estimate=pl.CostEstimate(
            flops=count * 2048, bytes_accessed=count * 1024, transcendentals=0
        ),
    )(filter_taps.reshape(count // LANES, 2 * LANES))


SHIFTS = 8
GROUPS = 8


def filter_kernel(signal_ref, taps_ref, out_ref, left, total):
    blocks = signal_ref.shape[0] - SHIFTS
    rows = blocks * 8
    steps = blocks // SHIFTS
    per = steps // GROUPS

    step = pl.program_id(0)

    def fill(i, carry):
        row = pl.multiple_of(i * LANES, LANES)
        for d in range(SHIFTS):
            left[pl.ds(row, LANES), d * LANES : (d + 1) * LANES] = (
                signal_ref[pl.ds(i * 16 + d, 16)].astype(F32).reshape(LANES, LANES).astype(BF16)
            )
        total[pl.ds(row, LANES), :] = jnp.zeros((LANES, 2 * LANES), F32)
        return carry

    @pl.when(step == 0)
    def _():
        lax.fori_loop(0, blocks // 16, fill, 0)
        left[rows:, :] = jnp.zeros_like(left[rows:, :])
        total[rows:, :] = jnp.zeros_like(total[rows:, :])

    for g in range(GROUPS):
        count = rows - g * per * SHIFTS * 8

        @pl.when(step // per == g)
        def _(count=count):
            a = left[pl.ds(pl.multiple_of(step * SHIFTS * 8, SHIFTS * 8), count), :]
            y = jnp.dot(a, taps_ref[...], preferred_element_type=F32)
            total[0:count, :] += y[:, : 2 * LANES] + y[:, 2 * LANES :]

    lane = lax.broadcasted_iota(jnp.int32, (8, LANES), 1)
    sublane = lax.broadcasted_iota(jnp.int32, (8, LANES), 0)
    _, y_count, z_count, c_count, x_count = out_ref.shape[:5]

    def finish(i, carry):
        yx, z = i // z_count, i % z_count
        y, x = yx // x_count, yx % x_count
        for c in range(c_count):
            row = pl.multiple_of((i * c_count + c) * 8, 8)
            same = total[pl.ds(row, 8), :LANES]
            cross = total[pl.ds(row, 8), LANES:]
            after = total[pl.ds(pl.multiple_of(row + 8, 8), 8), LANES:]
            moved = pltpu.roll(jnp.where(lane == 0, after, cross), LANES - 1, 1)
            other = pltpu.roll(jnp.where(sublane < 4, moved, cross), 4, 0)
            out_ref[0, y, z, c, x] = (same + other).astype(BF16)
            out_ref[1, y, z, c, x] = (same - other).astype(BF16)
        return carry

    @pl.when(step == steps - 1)
    def _():
        lax.fori_loop(0, blocks // c_count, finish, 0, unroll=4)


def filtered(signal, taps, sizes):
    s, yl, x, z, c = sizes
    blocks = signal.shape[0]
    padded = jnp.concatenate([signal, jnp.zeros((SHIFTS,) + signal.shape[1:], BF16)], 0)
    depth = SHIFTS * LANES
    return pl.pallas_call(
        filter_kernel,
        grid=(blocks // SHIFTS,),
        out_shape=jax.ShapeDtypeStruct((s, yl, z, c, x, 8, LANES), BF16),
        in_specs=[
            pl.BlockSpec(padded.shape, lambda i: (0, 0, 0)),
            pl.BlockSpec((depth, 4 * LANES), lambda i: (i, 0)),
        ],
        out_specs=pl.BlockSpec((s, yl, z, c, x, 8, LANES), lambda i: (0,) * 7),
        scratch_shapes=[
            pltpu.VMEM((blocks * 8 + LANES, depth), BF16),
            pltpu.VMEM((blocks * 8 + 8, 2 * LANES), F32),
        ],
        compiler_params=pltpu.CompilerParams(vmem_limit_bytes=24 << 20),
    )(padded, taps)


def along(array, axis, size, offset):
    return lax.ppermute(array, axis, [(i, (i + offset) % size) for i in range(size)])


def body(inputs, cotangent, weights, filter_taps):
    sizes = SIZES
    s, yl, x, z, c = sizes
    tokens, width = inputs.shape
    half = tokens // 2
    groups = yl * x * z * c
    sign, x_here, c_here = (lax.axis_index(name) for name in ("s", "x", "c"))
    row = lax.broadcasted_iota(jnp.int32, (tokens, tokens), 0)
    col = lax.broadcasted_iota(jnp.int32, (tokens, tokens), 1)
    order = (row == 2 * (col % half) + col // half).astype(BF16)
    taps = toeplitz(filter_taps)

    turned = lax.dot_general(
        cotangent, order, (((0,), (0,)), ((), ())), preferred_element_type=F32
    ).astype(BF16)
    chosen = lax.dynamic_index_in_dim(
        turned.reshape(groups, s, 4, 2, half), sign, 1, keepdims=False
    )
    send = chosen.transpose(0, 2, 1, 3).reshape(groups, 8, half)
    signal = lax.all_to_all(send, ("yl", "x", "z", "c"), split_axis=0, concat_axis=0, tiled=True)

    sorted_inputs = lax.dot_general(
        order, inputs, (((0,), (0,)), ((), ())), preferred_element_type=F32
    ).astype(BF16)
    gathered = [sorted_inputs] + [along(sorted_inputs, "x", x, k) for k in range(1, x)]
    split = weights[0].reshape(yl, x, z, c, s, 4, width)
    rows = jnp.stack(
        [lax.dynamic_index_in_dim(split, (x_here - k) % x, 1, keepdims=False) for k in range(x)]
    )
    rows = rows.transpose(0, 4, 1, 2, 3, 5, 6).reshape(width, width)

    signal, rows, gathered = lax.optimization_barrier((signal, rows, gathered))
    result = filtered(signal, taps, sizes).reshape(s * yl * z * c, x, 8, half)
    spread = lax.all_to_all(result, ("s", "yl", "z", "c"), split_axis=0, concat_axis=0, tiled=True)
    home = [
        along(
            lax.dynamic_index_in_dim(spread, (x_here + k) % x, 1, keepdims=False), "x", x, k
        )
        if k
        else lax.dynamic_index_in_dim(spread, x_here, 1, keepdims=False)
        for k in range(x)
    ]

    partial = 0
    for k in range(x):
        block = lax.dynamic_index_in_dim(spread, (x_here - k) % x, 1, keepdims=False)
        partial = partial + jnp.einsum(
            "qpka,pae->qke",
            block.reshape(s * yl * z * c, 2, 4, half),
            gathered[k].reshape(2, half, width),
            preferred_element_type=F32,
        )
    partial = partial.reshape(s, yl, z, c, 4, width).transpose(3, 1, 2, 0, 4, 5)
    partial = partial.reshape(c, yl * z, 8, width)
    other = lax.dynamic_index_in_dim(partial, 1 - c_here, 0, keepdims=False).astype(BF16)
    own = lax.dynamic_index_in_dim(partial, c_here, 0, keepdims=False)
    reduced = own + along(other, "c", c, 1).astype(F32)
    pieces = lax.all_to_all(
        reduced.astype(BF16), ("yl", "z"), split_axis=0, concat_axis=0, tiled=True
    )
    grad_scale = 1.0 / math.sqrt(tokens * groups)
    weight_grad = jnp.sum(pieces.astype(F32), 0) * grad_scale

    columns = jnp.stack(home).reshape(groups * s, 2, 4, half).transpose(1, 0, 2, 3)
    columns = columns.reshape(2, width, half)

    def project(side):
        matrix = lax.dynamic_slice_in_dim(rows, side * (width // 2), width // 2, 1)
        return jnp.einsum("pda,de->pae", columns, matrix, preferred_element_type=F32).astype(BF16)

    arrived = along(project(1 - sign), "s", s, 1)
    both = jnp.stack([project(sign), arrived]).reshape(2, tokens, width // 2)
    input_grad = jnp.einsum("tu,nue->te", order, both, preferred_element_type=F32).astype(BF16)
    return input_grad, weight_grad[None]


def solution(mesh):
    fine = Mesh(mesh.devices.reshape(SIZES), AXES)
    context = ("yl", "x", "z", "c")
    in_specs = (P(context, None), P(context, None), P("s", None, None), P())
    out_specs = (P(context, "s"), P("s", context, None))
    return jax.shard_map(body, mesh=fine, in_specs=in_specs, out_specs=out_specs, check_vma=False)
```

```python
import math

import jax
import jax.numpy as jnp
from jax import lax
from jax.experimental import pallas as pl
from jax.experimental.pallas import tpu as pltpu
from jax.sharding import Mesh, PartitionSpec as P

BF16, F32 = jnp.bfloat16, jnp.float32
LANES = 128
AXES = ("s", "yl", "x", "z", "c")
SIZES = (2, 2, 4, 8, 2)
VMEM = pl.BlockSpec(memory_space=pltpu.VMEM)
ANY = pl.BlockSpec(memory_space=pl.ANY)


def toeplitz_kernel(taps_ref, out_ref, rows):
    blocks = out_ref.shape[0] // LANES
    source = lax.broadcasted_iota(jnp.int32, (2 * LANES, 2 * LANES), 0)
    target = lax.broadcasted_iota(jnp.int32, (2 * LANES, 2 * LANES), 1)
    select = source == 2 * (LANES - 1 - target % LANES) + target // LANES

    @pl.when(pl.program_id(0) == 0)
    def _():
        chosen = sum(
            jnp.dot(
                taps_ref[pl.ds(n, taps_ref.shape[0] // 2, stride=2), :],
                select[n * LANES : (n + 1) * LANES].astype(F32),
                precision=lax.Precision.HIGHEST,
                preferred_element_type=F32,
            )
            for n in range(2)
        )
        for parity in range(2):
            rows[parity, 0:8, :] = jnp.zeros((8, LANES), F32)
            rows[parity, 8:, :] = chosen[:, parity * LANES : (parity + 1) * LANES]

    keep = lax.broadcasted_iota(jnp.int32, (LANES, LANES), 1) < LANES - 1 - lax.broadcasted_iota(
        jnp.int32, (LANES, LANES), 0
    )
    first = pl.program_id(0) * blocks

    def body(m, carry):
        row = pl.multiple_of(m * LANES, LANES)
        for parity in range(2):
            before = jnp.broadcast_to(rows[parity, pl.ds(first + m + 7, 1), :], (LANES, LANES))
            here = jnp.broadcast_to(rows[parity, pl.ds(first + m + 8, 1), :], (LANES, LANES))
            tile = pltpu.roll(jnp.where(keep, before, here), 1, 1, stride=1, stride_axis=0)
            high = tile.astype(BF16)
            out_ref[pl.ds(row, LANES), parity * LANES : (parity + 1) * LANES] = high
            out_ref[pl.ds(row, LANES), (2 + parity) * LANES : (3 + parity) * LANES] = (
                tile - high.astype(F32)
            ).astype(BF16)
        return carry

    lax.fori_loop(0, blocks, body, 0, unroll=8)


def toeplitz(filter_taps):
    count = filter_taps.shape[0] // 2
    parts = 4
    return pl.pallas_call(
        toeplitz_kernel,
        grid=(parts,),
        out_shape=jax.ShapeDtypeStruct((count, 4 * LANES), BF16),
        in_specs=[pl.BlockSpec((2 * count // LANES, LANES), lambda i: (0, 0))],
        out_specs=pl.BlockSpec((count // parts, 4 * LANES), lambda i: (i, 0)),
        scratch_shapes=[pltpu.VMEM((2, count // LANES + 8, LANES), F32)],
        compiler_params=pltpu.CompilerParams(vmem_limit_bytes=52 << 20),
        cost_estimate=pl.CostEstimate(
            flops=count * 2048, bytes_accessed=count * 1024, transcendentals=0
        ),
    )(filter_taps.reshape(2 * count // LANES, LANES))


SHIFTS = 16
GROUPS = 8


def filter_kernel(signal_ref, taps_ref, out_ref, held, left, total, table, arrived):
    blocks = signal_ref.shape[0]
    rows = blocks * 8
    steps = blocks // SHIFTS
    per = steps // GROUPS
    depth = SHIFTS * LANES

    def fetch(step):
        part = pl.ds(pl.multiple_of(step * depth, depth), depth)
        return pltpu.make_async_copy(taps_ref.at[part, :], table.at[part, :], arrived.at[step])

    def start(step, carry):
        fetch(step).start()
        return carry

    lax.fori_loop(0, steps, start, 0)

    held[:rows, :] = signal_ref[...].astype(F32).reshape(rows, LANES)
    held[rows:, :] = jnp.zeros((SHIFTS * 8, LANES), F32)

    def fill(i, carry):
        row = pl.multiple_of(i * LANES, LANES)
        for d in range(SHIFTS):
            left[pl.ds(row, LANES), d * LANES : (d + 1) * LANES] = held[
                pl.ds(pl.multiple_of(row + 8 * d, 8), LANES), :
            ].astype(BF16)
        total[pl.ds(row, LANES), :] = jnp.zeros((LANES, 2 * LANES), F32)
        return carry

    lax.fori_loop(0, rows // LANES, fill, 0)
    total[rows:, :] = jnp.zeros((8, 2 * LANES), F32)
    for g in range(GROUPS):
        count = rows - g * per * SHIFTS * 8

        def multiply(j, carry, g=g, count=count):
            step = g * per + j
            fetch(step).wait()
            a = left[pl.ds(pl.multiple_of(step * SHIFTS * 8, SHIFTS * 8), count), :]
            t = table[pl.ds(pl.multiple_of(step * depth, depth), depth), :]
            y = jnp.dot(a, t, preferred_element_type=F32)
            total[0:count, :] += y[:, : 2 * LANES] + y[:, 2 * LANES :]
            return carry

        lax.fori_loop(0, per * (1 + pl.program_id(0)), multiply, 0)

    lane = lax.broadcasted_iota(jnp.int32, (8, LANES), 1)
    sublane = lax.broadcasted_iota(jnp.int32, (8, LANES), 0)
    _, y_count, z_count, c_count, x_count = out_ref.shape[:5]

    def finish(i, carry):
        yx, z = i // z_count, i % z_count
        y, x = yx // x_count, yx % x_count
        for c in range(c_count):
            row = pl.multiple_of((i * c_count + c) * 8, 8)
            same = total[pl.ds(row, 8), :LANES]
            cross = total[pl.ds(row, 8), LANES:]
            after = total[pl.ds(pl.multiple_of(row + 8, 8), 8), LANES:]
            moved = pltpu.roll(jnp.where(lane == 0, after, cross), LANES - 1, 1)
            other = pltpu.roll(jnp.where(sublane < 4, moved, cross), 4, 0)
            out_ref[0, y, z, c, x] = (same + other).astype(BF16)
            out_ref[1, y, z, c, x] = (same - other).astype(BF16)
        return carry

    lax.fori_loop(0, blocks // c_count, finish, 0, unroll=4)


def filtered(signal, taps, sizes):
    s, yl, x, z, c = sizes
    blocks = signal.shape[0]
    depth = SHIFTS * LANES
    return pl.pallas_call(
        filter_kernel,
        grid=(1,),
        out_shape=jax.ShapeDtypeStruct((s, yl, z, c, x, 8, LANES), BF16),
        in_specs=[VMEM, ANY],
        out_specs=VMEM,
        scratch_shapes=[
            pltpu.VMEM(((blocks + SHIFTS) * 8, LANES), F32),
            pltpu.VMEM((blocks * 8, depth), BF16),
            pltpu.VMEM((blocks * 8 + 8, 2 * LANES), F32),
            pltpu.VMEM(taps.shape, BF16),
            pltpu.SemaphoreType.DMA((blocks // SHIFTS,)),
        ],
        compiler_params=pltpu.CompilerParams(vmem_limit_bytes=52 << 20),
        cost_estimate=pl.CostEstimate(
            flops=blocks * 8 * depth * blocks * LANES * 8 // 8,
            bytes_accessed=taps.shape[0] * taps.shape[1] * 2,
            transcendentals=0,
        ),
    )(signal, taps)


def along(array, axis, size, offset):
    return lax.ppermute(array, axis, [(i, (i + offset) % size) for i in range(size)])


TURN_PARTS = 4


def turn_kernel(order_ref, cotangent_ref, out_ref, held, turned, arrived):
    width = held.shape[1]
    part = width // TURN_PARTS
    copies = [
        pltpu.make_async_copy(
            cotangent_ref.at[:, n * part : (n + 1) * part],
            held.at[:, n * part : (n + 1) * part],
            arrived.at[n],
        )
        for n in range(TURN_PARTS)
    ]
    for copy in copies:
        copy.start()
    sign = lax.axis_index("s")
    upper = lax.broadcasted_iota(jnp.int32, (8, LANES), 0) < 4

    def place(i, carry):
        row = pl.multiple_of(i * 8, 8)
        even, odd = turned[pl.ds(row, 8), :LANES], turned[pl.ds(row, 8), LANES:]
        lower_rows = jnp.where(upper, even, pltpu.roll(odd, 4, 0))
        upper_rows = jnp.where(upper, pltpu.roll(even, 4, 0), odd)
        out_ref[i] = jnp.where(sign == 0, lower_rows, upper_rows).astype(BF16)
        return carry

    for n in range(TURN_PARTS):
        copies[n].wait()
        turned[n * part : (n + 1) * part, :] = lax.dot_general(
            held[:, n * part : (n + 1) * part],
            order_ref[...],
            (((0,), (0,)), ((), ())),
            preferred_element_type=F32,
        )
        lax.fori_loop(n * part // 8, (n + 1) * part // 8, place, 0, unroll=8)


def turn(order, cotangent):
    tokens, width = cotangent.shape
    return pl.pallas_call(
        turn_kernel,
        out_shape=jax.ShapeDtypeStruct((width // 8, 8, tokens // 2), BF16),
        in_specs=[VMEM, ANY],
        out_specs=VMEM,
        scratch_shapes=[
            pltpu.VMEM((tokens, width), BF16),
            pltpu.VMEM((width, tokens), F32),
            pltpu.SemaphoreType.DMA((TURN_PARTS,)),
        ],
        compiler_params=pltpu.CompilerParams(vmem_limit_bytes=16 << 20),
    )(order, cotangent)


def pair(first, second, upper):
    first, second = first.astype(F32), second.astype(F32)
    even = jnp.where(upper, first, pltpu.roll(second, 4, 0))
    odd = jnp.where(upper, pltpu.roll(first, 4, 0), second)
    return even.astype(BF16), odd.astype(BF16)


def weight_kernel(spread_ref, *refs):
    *gathered, own_ref, other_ref, left, right, arrived = refs
    x = spread_ref.shape[1]
    half = spread_ref.shape[0] // 2
    tiles = half // 2
    tokens = right.shape[0] // x
    x_here, c_here = lax.axis_index("x"), lax.axis_index("c")
    upper = lax.broadcasted_iota(jnp.int32, (8, LANES), 0) < 4
    copies, row = [], 0
    for n, ref in enumerate(gathered):
        copies.append(
            pltpu.make_async_copy(ref, right.at[row : row + ref.shape[0], :], arrived.at[n])
        )
        row += ref.shape[0]
    for copy in copies:
        copy.start()
    for k in range(x):
        block = lax.rem(x_here - k + x, x)
        for part in range(2):
            core = c_here if part == 0 else 1 - c_here

            def place(i, carry, k=k, block=block, part=part, core=core):
                pairs = [
                    pair(
                        spread_ref[2 * (2 * i + n) + core, block],
                        spread_ref[half + 2 * (2 * i + n) + core, block],
                        upper,
                    )
                    for n in range(2)
                ]
                at = pl.multiple_of(part * tiles * 8 + i * 16, 16)
                for parity in range(2):
                    col = k * tokens + parity * LANES
                    left[pl.ds(at, 16), col : col + LANES] = jnp.concatenate(
                        [pairs[0][parity], pairs[1][parity]], 0
                    )
                return carry

            lax.fori_loop(0, tiles // 2, place, 0, unroll=4)
    for copy in copies:
        copy.wait()
    y = jnp.dot(left[...], right[...], preferred_element_type=F32)
    own_ref[...] = y[: tiles * 8, :]
    other_ref[...] = y[tiles * 8 :, :].astype(BF16)


def weight_part(spread, gathered):
    count, x = spread.shape[:2]
    tokens, width = gathered[0].shape
    rows = count * 4
    return pl.pallas_call(
        weight_kernel,
        out_shape=[
            jax.ShapeDtypeStruct((rows // 2, width), F32),
            jax.ShapeDtypeStruct((rows // 2, width), BF16),
        ],
        in_specs=[VMEM] + [ANY] * len(gathered),
        out_specs=[VMEM, VMEM],
        scratch_shapes=[
            pltpu.VMEM((rows, x * tokens), BF16),
            pltpu.VMEM((x * tokens, width), BF16),
            pltpu.SemaphoreType.DMA((len(gathered),)),
        ],
        compiler_params=pltpu.CompilerParams(vmem_limit_bytes=60 << 20),
        cost_estimate=pl.CostEstimate(
            flops=2 * rows * x * tokens * width,
            bytes_accessed=4 * x * tokens * width,
            transcendentals=0,
        ),
    )(spread, *gathered)


def project_kernel(order_ref, weights_ref, *refs):
    *home, mine_ref, theirs_ref, columns, part, matrix, arrived = refs
    copy = pltpu.make_async_copy(weights_ref, matrix, arrived)
    copy.start()
    x = len(home)
    half = home[0].shape[0] // 2
    width = weights_ref.shape[0]
    yl = width // (LANES * x)
    x_here, sign = lax.axis_index("x"), lax.axis_index("s")
    upper = lax.broadcasted_iota(jnp.int32, (8, LANES), 0) < 4
    per = half // yl
    for k in range(x):
        block = lax.rem(x_here - k + x, x)
        for y in range(yl):

            def place(i, carry, k=k, y=y, block=block):
                q = y * per + 2 * i
                tile_pairs = [
                    pair(home[k][q + n], home[k][half + q + n], upper) for n in range(2)
                ]
                row = pl.multiple_of((y * x + block) * LANES + i * 16, 16)
                for parity in range(2):
                    columns[pl.ds(row, 16), parity * LANES : (parity + 1) * LANES] = (
                        jnp.concatenate([tile_pairs[0][parity], tile_pairs[1][parity]], 0)
                    )
                return carry

            lax.fori_loop(0, per // 2, place, 0, unroll=4)
    copy.wait()
    part[...] = lax.dot_general(
        columns[...], matrix[...], (((0,), (0,)), ((), ())), preferred_element_type=F32
    ).astype(BF16)
    whole = jnp.dot(order_ref[...], part[...], preferred_element_type=F32).astype(BF16)
    side = width // 2

    @pl.when(sign == 0)
    def _():
        mine_ref[...] = whole[:, :side]
        theirs_ref[...] = whole[:, side:]

    @pl.when(sign == 1)
    def _():
        mine_ref[...] = whole[:, side:]
        theirs_ref[...] = whole[:, :side]


def project(order, weights, home):
    tokens, width = order.shape[0], weights.shape[0]
    return pl.pallas_call(
        project_kernel,
        out_shape=[jax.ShapeDtypeStruct((tokens, width // 2), BF16)] * 2,
        in_specs=[VMEM, ANY] + [VMEM] * len(home),
        out_specs=[VMEM, VMEM],
        scratch_shapes=[
            pltpu.VMEM((width, tokens), BF16),
            pltpu.VMEM((tokens, width), BF16),
            pltpu.VMEM((width, width), BF16),
            pltpu.SemaphoreType.DMA,
        ],
        compiler_params=pltpu.CompilerParams(vmem_limit_bytes=24 << 20),
        cost_estimate=pl.CostEstimate(
            flops=2 * tokens * width * width, bytes_accessed=4 * width * width, transcendentals=0
        ),
    )(order, weights, *home)


def body(inputs, cotangent, weights, filter_taps):
    sizes = SIZES
    s, yl, x, z, c = sizes
    tokens, width = inputs.shape
    half = tokens // 2
    groups = yl * x * z * c
    x_here = lax.axis_index("x")
    row = lax.broadcasted_iota(jnp.int32, (tokens, tokens), 0)
    col = lax.broadcasted_iota(jnp.int32, (tokens, tokens), 1)
    order = (row == 2 * (col % half) + col // half).astype(BF16)

    send = turn(order, cotangent)
    signal = lax.all_to_all(send, ("yl", "x", "z", "c"), split_axis=0, concat_axis=0, tiled=True)

    taps = toeplitz(filter_taps)
    taps, inputs = lax.optimization_barrier((taps, inputs))
    sorted_inputs = lax.dot_general(
        order, inputs, (((0,), (0,)), ((), ())), preferred_element_type=F32
    ).astype(BF16)
    before, after = along(sorted_inputs, "x", x, 1), along(sorted_inputs, "x", x, x - 1)

    result = filtered(signal, taps, sizes).reshape(s * yl * z * c, x, 8, half)
    result, before, after = lax.optimization_barrier((result, before, after))
    gathered = [
        sorted_inputs,
        before,
        along(before[:half], "x", x, 1),
        along(after[half:], "x", x, x - 1),
        after,
    ]
    spread = lax.all_to_all(result, ("s", "yl", "z", "c"), split_axis=0, concat_axis=0, tiled=True)
    home = [
        lax.dynamic_index_in_dim(spread, lax.rem(x_here + k, x), 1, keepdims=False)
        for k in range(x)
    ]

    spread, *home = lax.optimization_barrier((spread, *home))
    home = [home[0]] + [along(home[k], "x", x, k) for k in range(1, x)]
    own, other = weight_part(spread, gathered)
    other, *home = lax.optimization_barrier((other, *home))
    other = along(other, "c", c, 1)
    mine, theirs = project(order, weights[0], home)
    reduced = (own + other.astype(F32)).astype(BF16).reshape(yl * z, 8, width)
    theirs, reduced = lax.optimization_barrier((theirs, reduced))
    arrived = along(theirs, "s", s, 1)
    pieces = lax.all_to_all(reduced, ("yl", "z"), split_axis=0, concat_axis=0, tiled=True)
    grad_scale = 1.0 / math.sqrt(tokens * groups)
    weight_grad = jnp.sum(pieces.astype(F32), 0) * grad_scale
    input_grad = (mine.astype(F32) + arrived.astype(F32)).astype(BF16)
    return input_grad, weight_grad[None]


def solution(mesh):
    fine = Mesh(mesh.devices.reshape(SIZES), AXES)
    context = ("yl", "x", "z", "c")
    in_specs = (P(context, None), P(context, None), P("s", None, None), P())
    out_specs = (P(context, "s"), P("s", context, None))
    return jax.shard_map(body, mesh=fine, in_specs=in_specs, out_specs=out_specs, check_vma=False)
```

```python
import math

import jax
import jax.numpy as jnp
from jax import lax
from jax.experimental import pallas as pl
from jax.experimental.pallas import tpu as pltpu
from jax.sharding import Mesh, PartitionSpec as P

BF16, F32 = jnp.bfloat16, jnp.float32
LANES = 128
AXES = ("s", "yl", "x", "z", "c")
SIZES = (2, 2, 4, 8, 2)
VMEM = pl.BlockSpec(memory_space=pltpu.VMEM)
ANY = pl.BlockSpec(memory_space=pl.ANY)


def toeplitz_kernel(taps_ref, out_ref, rows):
    blocks = out_ref.shape[0] // LANES
    source = lax.broadcasted_iota(jnp.int32, (2 * LANES, 2 * LANES), 0)
    target = lax.broadcasted_iota(jnp.int32, (2 * LANES, 2 * LANES), 1)
    select = source == 2 * (LANES - 1 - target % LANES) + target // LANES

    @pl.when(pl.program_id(0) == 0)
    def _():
        chosen = sum(
            jnp.dot(
                taps_ref[pl.ds(n, taps_ref.shape[0] // 2, stride=2), :],
                select[n * LANES : (n + 1) * LANES].astype(F32),
                precision=lax.Precision.HIGHEST,
                preferred_element_type=F32,
            )
            for n in range(2)
        )
        for parity in range(2):
            rows[parity, 0:8, :] = jnp.zeros((8, LANES), F32)
            rows[parity, 8:, :] = chosen[:, parity * LANES : (parity + 1) * LANES]

    keep = lax.broadcasted_iota(jnp.int32, (LANES, LANES), 1) < LANES - 1 - lax.broadcasted_iota(
        jnp.int32, (LANES, LANES), 0
    )
    first = pl.program_id(0) * blocks

    def body(m, carry):
        row = pl.multiple_of(m * LANES, LANES)
        for parity in range(2):
            before = jnp.broadcast_to(rows[parity, pl.ds(first + m + 7, 1), :], (LANES, LANES))
            here = jnp.broadcast_to(rows[parity, pl.ds(first + m + 8, 1), :], (LANES, LANES))
            tile = pltpu.roll(jnp.where(keep, before, here), 1, 1, stride=1, stride_axis=0)
            high = tile.astype(BF16)
            out_ref[pl.ds(row, LANES), parity * LANES : (parity + 1) * LANES] = high
            out_ref[pl.ds(row, LANES), (2 + parity) * LANES : (3 + parity) * LANES] = (
                tile - high.astype(F32)
            ).astype(BF16)
        return carry

    lax.fori_loop(0, blocks, body, 0, unroll=8)


def toeplitz(filter_taps):
    count = filter_taps.shape[0] // 2
    parts = 4
    return pl.pallas_call(
        toeplitz_kernel,
        grid=(parts,),
        out_shape=jax.ShapeDtypeStruct((count, 4 * LANES), BF16),
        in_specs=[pl.BlockSpec((2 * count // LANES, LANES), lambda i: (0, 0))],
        out_specs=pl.BlockSpec((count // parts, 4 * LANES), lambda i: (i, 0)),
        scratch_shapes=[pltpu.VMEM((2, count // LANES + 8, LANES), F32)],
        compiler_params=pltpu.CompilerParams(vmem_limit_bytes=52 << 20),
        cost_estimate=pl.CostEstimate(
            flops=count * 2048, bytes_accessed=count * 1024, transcendentals=0
        ),
    )(filter_taps.reshape(2 * count // LANES, LANES))


SHIFTS = 16
GROUPS = 8


def filter_kernel(signal_ref, taps_ref, out_ref, held, left, total, table, arrived):
    blocks = signal_ref.shape[0]
    rows = blocks * 8
    steps = blocks // SHIFTS
    per = steps // GROUPS
    depth = SHIFTS * LANES

    def fetch(step):
        part = pl.ds(pl.multiple_of(step * depth, depth), depth)
        return pltpu.make_async_copy(taps_ref.at[part, :], table.at[part, :], arrived.at[step])

    def start(step, carry):
        fetch(step).start()
        return carry

    lax.fori_loop(0, steps, start, 0)

    held[:rows, :] = signal_ref[...].astype(F32).reshape(rows, LANES)
    held[rows:, :] = jnp.zeros((SHIFTS * 8, LANES), F32)

    def fill(i, carry):
        row = pl.multiple_of(i * LANES, LANES)
        for d in range(SHIFTS):
            left[pl.ds(row, LANES), d * LANES : (d + 1) * LANES] = held[
                pl.ds(pl.multiple_of(row + 8 * d, 8), LANES), :
            ].astype(BF16)
        total[pl.ds(row, LANES), :] = jnp.zeros((LANES, 2 * LANES), F32)
        return carry

    lax.fori_loop(0, rows // LANES, fill, 0)
    total[rows:, :] = jnp.zeros((8, 2 * LANES), F32)
    for g in range(GROUPS):
        count = rows - g * per * SHIFTS * 8

        def multiply(j, carry, g=g, count=count):
            step = g * per + j
            fetch(step).wait()
            a = left[pl.ds(pl.multiple_of(step * SHIFTS * 8, SHIFTS * 8), count), :]
            t = table[pl.ds(pl.multiple_of(step * depth, depth), depth), :]
            y = jnp.dot(a, t, preferred_element_type=F32)
            total[0:count, :] += y[:, : 2 * LANES] + y[:, 2 * LANES :]
            return carry

        lax.fori_loop(0, per * (1 + pl.program_id(0)), multiply, 0)

    lane = lax.broadcasted_iota(jnp.int32, (8, LANES), 1)
    sublane = lax.broadcasted_iota(jnp.int32, (8, LANES), 0)
    _, y_count, z_count, c_count, x_count = out_ref.shape[:5]

    def finish(i, carry):
        yx, z = i // z_count, i % z_count
        y, x = yx // x_count, yx % x_count
        for c in range(c_count):
            row = pl.multiple_of((i * c_count + c) * 8, 8)
            same = total[pl.ds(row, 8), :LANES]
            cross = total[pl.ds(row, 8), LANES:]
            after = total[pl.ds(pl.multiple_of(row + 8, 8), 8), LANES:]
            moved = pltpu.roll(jnp.where(lane == 0, after, cross), LANES - 1, 1)
            other = pltpu.roll(jnp.where(sublane < 4, moved, cross), 4, 0)
            out_ref[0, y, z, c, x] = (same + other).astype(BF16)
            out_ref[1, y, z, c, x] = (same - other).astype(BF16)
        return carry

    lax.fori_loop(0, blocks // c_count, finish, 0, unroll=4)


def filtered(signal, taps, sizes):
    s, yl, x, z, c = sizes
    blocks = signal.shape[0]
    depth = SHIFTS * LANES
    return pl.pallas_call(
        filter_kernel,
        grid=(1,),
        out_shape=jax.ShapeDtypeStruct((s, yl, z, c, x, 8, LANES), BF16),
        in_specs=[VMEM, ANY],
        out_specs=VMEM,
        scratch_shapes=[
            pltpu.VMEM(((blocks + SHIFTS) * 8, LANES), F32),
            pltpu.VMEM((blocks * 8, depth), BF16),
            pltpu.VMEM((blocks * 8 + 8, 2 * LANES), F32),
            pltpu.VMEM(taps.shape, BF16),
            pltpu.SemaphoreType.DMA((blocks // SHIFTS,)),
        ],
        compiler_params=pltpu.CompilerParams(vmem_limit_bytes=52 << 20),
        cost_estimate=pl.CostEstimate(
            flops=blocks * 8 * depth * blocks * LANES * 8 // 8,
            bytes_accessed=taps.shape[0] * taps.shape[1] * 2,
            transcendentals=0,
        ),
    )(signal, taps)


def along(array, axis, size, offset):
    return lax.ppermute(array, axis, [(i, (i + offset) % size) for i in range(size)])


def turn_kernel(order_ref, cotangent_ref, out_ref, turned):
    turned[...] = lax.dot_general(
        cotangent_ref[...], order_ref[...], (((0,), (0,)), ((), ())), preferred_element_type=F32
    )
    sign = lax.axis_index("s")
    upper = lax.broadcasted_iota(jnp.int32, (8, LANES), 0) < 4

    def place(i, carry):
        row = pl.multiple_of(i * 8, 8)
        even, odd = turned[pl.ds(row, 8), :LANES], turned[pl.ds(row, 8), LANES:]
        lower_rows = jnp.where(upper, even, pltpu.roll(odd, 4, 0))
        upper_rows = jnp.where(upper, pltpu.roll(even, 4, 0), odd)
        out_ref[i] = jnp.where(sign == 0, lower_rows, upper_rows).astype(BF16)
        return carry

    lax.fori_loop(0, out_ref.shape[0], place, 0, unroll=8)


def turn(order, cotangent):
    tokens, width = cotangent.shape
    return pl.pallas_call(
        turn_kernel,
        out_shape=jax.ShapeDtypeStruct((width // 8, 8, tokens // 2), BF16),
        in_specs=[VMEM, VMEM],
        out_specs=VMEM,
        scratch_shapes=[pltpu.VMEM((width, tokens), F32)],
        compiler_params=pltpu.CompilerParams(vmem_limit_bytes=16 << 20),
    )(order, cotangent)


def pair(first, second, upper):
    first, second = first.astype(F32), second.astype(F32)
    even = jnp.where(upper, first, pltpu.roll(second, 4, 0))
    odd = jnp.where(upper, pltpu.roll(first, 4, 0), second)
    return even.astype(BF16), odd.astype(BF16)


def weight_kernel(order_ref, spread_ref, *refs):
    *gathered, own_ref, other_ref, blocks, left, turned, right, sent, arrived = refs
    x = blocks.shape[0]
    half = blocks.shape[1] // 2
    tiles = half // 2
    tokens = right.shape[0] // x
    x_here, c_here = lax.axis_index("x"), lax.axis_index("c")
    upper = lax.broadcasted_iota(jnp.int32, (8, LANES), 0) < 4
    fetches, copies, row = [], [], 0
    for k in range(x):
        block = lax.rem(x_here - k + x, x)
        fetches.append(pltpu.make_async_copy(spread_ref.at[:, block], blocks.at[k], sent.at[k]))
        fetches[k].start()
    for n, ref in enumerate(gathered):
        copies.append(
            pltpu.make_async_copy(ref, right.at[row : row + ref.shape[0], :], arrived.at[n])
        )
        row += ref.shape[0]
        copies[n].start()
    for k in range(x):
        fetches[k].wait()
        for part in range(2):
            core = c_here if part == 0 else 1 - c_here

            def place(i, carry, k=k, part=part, core=core):
                pairs = [
                    pair(
                        blocks[k, 2 * (2 * i + n) + core],
                        blocks[k, half + 2 * (2 * i + n) + core],
                        upper,
                    )
                    for n in range(2)
                ]
                at = pl.multiple_of(part * tiles * 8 + i * 16, 16)
                for parity in range(2):
                    left[pl.ds(at, 16), parity * LANES : (parity + 1) * LANES] = (
                        jnp.concatenate([pairs[0][parity], pairs[1][parity]], 0)
                    )
                return carry

            lax.fori_loop(0, tiles // 2, place, 0, unroll=4)
        turned[:, k * tokens : (k + 1) * tokens] = lax.dot_general(
            left[...], order_ref[...], (((1,), (1,)), ((), ())), preferred_element_type=F32
        ).astype(BF16)
    for copy in copies:
        copy.wait()
    y = jnp.dot(turned[...], right[...], preferred_element_type=F32).astype(BF16)
    own_ref[...] = y[: tiles * 8, :]
    other_ref[...] = y[tiles * 8 :, :]


def weight_part(order, spread, gathered):
    count, x = spread.shape[:2]
    tokens, width = gathered[0].shape
    rows = count * 4
    return pl.pallas_call(
        weight_kernel,
        out_shape=[jax.ShapeDtypeStruct((rows // 2, width), BF16)] * 2,
        in_specs=[VMEM] + [ANY] * (1 + len(gathered)),
        out_specs=[VMEM, VMEM],
        scratch_shapes=[
            pltpu.VMEM((x, count, 8, LANES), BF16),
            pltpu.VMEM((rows, tokens), BF16),
            pltpu.VMEM((rows, x * tokens), BF16),
            pltpu.VMEM((x * tokens, width), BF16),
            pltpu.SemaphoreType.DMA((x,)),
            pltpu.SemaphoreType.DMA((len(gathered),)),
        ],
        compiler_params=pltpu.CompilerParams(vmem_limit_bytes=24 << 20),
        cost_estimate=pl.CostEstimate(
            flops=2 * rows * x * tokens * width,
            bytes_accessed=4 * x * tokens * width,
            transcendentals=0,
        ),
    )(order, spread, *gathered)


def project_kernel(order_ref, weights_ref, *refs):
    *home, mine_ref, theirs_ref, columns, part, matrix, arrived = refs
    copy = pltpu.make_async_copy(weights_ref, matrix, arrived)
    copy.start()
    x = len(home)
    half = home[0].shape[0] // 2
    width = weights_ref.shape[0]
    yl = width // (LANES * x)
    x_here, sign = lax.axis_index("x"), lax.axis_index("s")
    upper = lax.broadcasted_iota(jnp.int32, (8, LANES), 0) < 4
    per = half // yl
    for k in range(x):
        block = lax.rem(x_here - k + x, x)
        for y in range(yl):

            def place(i, carry, k=k, y=y, block=block):
                q = y * per + 2 * i
                tile_pairs = [
                    pair(home[k][q + n], home[k][half + q + n], upper) for n in range(2)
                ]
                row = pl.multiple_of((y * x + block) * LANES + i * 16, 16)
                for parity in range(2):
                    columns[pl.ds(row, 16), parity * LANES : (parity + 1) * LANES] = (
                        jnp.concatenate([tile_pairs[0][parity], tile_pairs[1][parity]], 0)
                    )
                return carry

            lax.fori_loop(0, per // 2, place, 0, unroll=4)
    copy.wait()
    part[...] = lax.dot_general(
        columns[...], matrix[...], (((0,), (0,)), ((), ())), preferred_element_type=F32
    ).astype(BF16)
    whole = jnp.dot(order_ref[...], part[...], preferred_element_type=F32).astype(BF16)
    side = width // 2

    @pl.when(sign == 0)
    def _():
        mine_ref[...] = whole[:, :side]
        theirs_ref[...] = whole[:, side:]

    @pl.when(sign == 1)
    def _():
        mine_ref[...] = whole[:, side:]
        theirs_ref[...] = whole[:, :side]


def project(order, weights, home):
    tokens, width = order.shape[0], weights.shape[0]
    return pl.pallas_call(
        project_kernel,
        out_shape=[jax.ShapeDtypeStruct((tokens, width // 2), BF16)] * 2,
        in_specs=[VMEM, ANY] + [VMEM] * len(home),
        out_specs=[VMEM, VMEM],
        scratch_shapes=[
            pltpu.VMEM((width, tokens), BF16),
            pltpu.VMEM((tokens, width), BF16),
            pltpu.VMEM((width, width), BF16),
            pltpu.SemaphoreType.DMA,
        ],
        compiler_params=pltpu.CompilerParams(vmem_limit_bytes=24 << 20),
        cost_estimate=pl.CostEstimate(
            flops=2 * tokens * width * width, bytes_accessed=4 * width * width, transcendentals=0
        ),
    )(order, weights, *home)


def body(inputs, cotangent, weights, filter_taps):
    sizes = SIZES
    s, yl, x, z, c = sizes
    tokens, width = inputs.shape
    half = tokens // 2
    groups = yl * x * z * c
    x_here = lax.axis_index("x")
    row = lax.broadcasted_iota(jnp.int32, (tokens, tokens), 0)
    col = lax.broadcasted_iota(jnp.int32, (tokens, tokens), 1)
    order = (row == 2 * (col % half) + col // half).astype(BF16)

    send = turn(order, cotangent)
    signal = lax.all_to_all(send, ("yl", "x", "z", "c"), split_axis=0, concat_axis=0, tiled=True)

    taps = toeplitz(filter_taps)
    taps, inputs = lax.optimization_barrier((taps, inputs))
    before, after = along(inputs, "x", x, 1), along(inputs, "x", x, x - 1)

    result = filtered(signal, taps, sizes).reshape(s * yl * z * c, x, 8, half)
    result, before, after = lax.optimization_barrier((result, before, after))
    gathered = [
        inputs,
        before,
        along(before[:half], "x", x, 1),
        along(after[half:], "x", x, x - 1),
        after,
    ]
    spread = lax.all_to_all(result, ("s", "yl", "z", "c"), split_axis=0, concat_axis=0, tiled=True)
    home = [
        lax.dynamic_index_in_dim(spread, lax.rem(x_here + k, x), 1, keepdims=False)
        for k in range(x)
    ]

    own, other = weight_part(order, spread, gathered)
    other, *home = lax.optimization_barrier((other, *home))
    home = [home[0]] + [along(home[k], "x", x, k) for k in range(1, x)]
    other = along(other, "c", c, 1)
    reduced = (own.astype(F32) + other.astype(F32)).astype(BF16).reshape(yl * z, 8, width)
    _, *home = lax.optimization_barrier((reduced, *home))
    mine, theirs = project(order, weights[0], home)
    arrived = jnp.concatenate([along(theirs[:half], "s", s, 1), along(theirs[half:], "s", s, 1)])
    pieces = lax.all_to_all(reduced, ("yl", "z"), split_axis=0, concat_axis=0, tiled=True)
    grad_scale = 1.0 / math.sqrt(tokens * groups)
    weight_grad = jnp.sum(pieces.astype(F32), 0) * grad_scale
    input_grad = (mine.astype(F32) + arrived.astype(F32)).astype(BF16)
    return input_grad, weight_grad[None]


def solution(mesh):
    fine = Mesh(mesh.devices.reshape(SIZES), AXES)
    context = ("yl", "x", "z", "c")
    in_specs = (P(context, None), P(context, None), P("s", None, None), P())
    out_specs = (P(context, "s"), P("s", context, None))
    return jax.shard_map(body, mesh=fine, in_specs=in_specs, out_specs=out_specs, check_vma=False)
```

```python
import math

import jax
import jax.numpy as jnp
from jax import lax
from jax.experimental import pallas as pl
from jax.experimental.pallas import tpu as pltpu
from jax.sharding import Mesh, PartitionSpec as P

BF16, F32 = jnp.bfloat16, jnp.float32
LANES = 128
AXES = ("s", "yl", "x", "z", "c")
SIZES = (2, 2, 4, 8, 2)
VMEM = pl.BlockSpec(memory_space=pltpu.VMEM)
ANY = pl.BlockSpec(memory_space=pl.ANY)


def toeplitz_kernel(taps_ref, out_ref, rows):
    blocks = out_ref.shape[0] // LANES
    source = lax.broadcasted_iota(jnp.int32, (2 * LANES, 2 * LANES), 0)
    target = lax.broadcasted_iota(jnp.int32, (2 * LANES, 2 * LANES), 1)
    select = source == 2 * (LANES - 1 - target % LANES) + target // LANES

    @pl.when(pl.program_id(0) == 0)
    def _():
        chosen = sum(
            jnp.dot(
                taps_ref[pl.ds(n, taps_ref.shape[0] // 2, stride=2), :],
                select[n * LANES : (n + 1) * LANES].astype(F32),
                precision=lax.Precision.HIGHEST,
                preferred_element_type=F32,
            )
            for n in range(2)
        )
        for parity in range(2):
            rows[parity, 0:8, :] = jnp.zeros((8, LANES), F32)
            rows[parity, 8:, :] = chosen[:, parity * LANES : (parity + 1) * LANES]

    keep = lax.broadcasted_iota(jnp.int32, (LANES, LANES), 1) < LANES - 1 - lax.broadcasted_iota(
        jnp.int32, (LANES, LANES), 0
    )
    first = pl.program_id(0) * blocks

    def body(m, carry):
        row = pl.multiple_of(m * LANES, LANES)
        for parity in range(2):
            before = jnp.broadcast_to(rows[parity, pl.ds(first + m + 7, 1), :], (LANES, LANES))
            here = jnp.broadcast_to(rows[parity, pl.ds(first + m + 8, 1), :], (LANES, LANES))
            tile = pltpu.roll(jnp.where(keep, before, here), 1, 1, stride=1, stride_axis=0)
            high = tile.astype(BF16)
            out_ref[pl.ds(row, LANES), parity * LANES : (parity + 1) * LANES] = high
            out_ref[pl.ds(row, LANES), (2 + parity) * LANES : (3 + parity) * LANES] = (
                tile - high.astype(F32)
            ).astype(BF16)
        return carry

    lax.fori_loop(0, blocks, body, 0, unroll=8)


def toeplitz(filter_taps):
    count = filter_taps.shape[0] // 2
    parts = 4
    return pl.pallas_call(
        toeplitz_kernel,
        grid=(parts,),
        out_shape=jax.ShapeDtypeStruct((count, 4 * LANES), BF16),
        in_specs=[pl.BlockSpec((2 * count // LANES, LANES), lambda i: (0, 0))],
        out_specs=pl.BlockSpec((count // parts, 4 * LANES), lambda i: (i, 0)),
        scratch_shapes=[pltpu.VMEM((2, count // LANES + 8, LANES), F32)],
        compiler_params=pltpu.CompilerParams(vmem_limit_bytes=52 << 20),
        cost_estimate=pl.CostEstimate(
            flops=count * 2048, bytes_accessed=count * 1024, transcendentals=0
        ),
    )(filter_taps.reshape(2 * count // LANES, LANES))


SHIFTS = 16
GROUPS = 8


def filter_kernel(signal_ref, taps_ref, out_ref, held, left, total, table, arrived):
    blocks = signal_ref.shape[0]
    rows = blocks * 8
    steps = blocks // SHIFTS
    per = steps // GROUPS
    depth = SHIFTS * LANES

    def fetch(step):
        part = pl.ds(pl.multiple_of(step * depth, depth), depth)
        return pltpu.make_async_copy(taps_ref.at[part, :], table.at[part, :], arrived.at[step])

    def start(step, carry):
        fetch(step).start()
        return carry

    lax.fori_loop(0, steps, start, 0)

    held[:rows, :] = signal_ref[...].astype(F32).reshape(rows, LANES)
    held[rows:, :] = jnp.zeros((SHIFTS * 8, LANES), F32)

    def fill(i, carry):
        row = pl.multiple_of(i * LANES, LANES)
        for d in range(SHIFTS):
            left[pl.ds(row, LANES), d * LANES : (d + 1) * LANES] = held[
                pl.ds(pl.multiple_of(row + 8 * d, 8), LANES), :
            ].astype(BF16)
        total[pl.ds(row, LANES), :] = jnp.zeros((LANES, 2 * LANES), F32)
        return carry

    lax.fori_loop(0, rows // LANES, fill, 0)
    total[rows:, :] = jnp.zeros((8, 2 * LANES), F32)
    for g in range(GROUPS):
        count = rows - g * per * SHIFTS * 8

        def multiply(j, carry, g=g, count=count):
            step = g * per + j
            fetch(step).wait()
            a = left[pl.ds(pl.multiple_of(step * SHIFTS * 8, SHIFTS * 8), count), :]
            t = table[pl.ds(pl.multiple_of(step * depth, depth), depth), :]
            y = jnp.dot(a, t, preferred_element_type=F32)
            total[0:count, :] += y[:, : 2 * LANES] + y[:, 2 * LANES :]
            return carry

        lax.fori_loop(0, per * (1 + pl.program_id(0)), multiply, 0)

    lane = lax.broadcasted_iota(jnp.int32, (8, LANES), 1)
    sublane = lax.broadcasted_iota(jnp.int32, (8, LANES), 0)
    _, y_count, z_count, c_count, x_count = out_ref.shape[:5]

    def finish(i, carry):
        yx, z = i // z_count, i % z_count
        y, x = yx // x_count, yx % x_count
        for c in range(c_count):
            row = pl.multiple_of((i * c_count + c) * 8, 8)
            same = total[pl.ds(row, 8), :LANES]
            cross = total[pl.ds(row, 8), LANES:]
            after = total[pl.ds(pl.multiple_of(row + 8, 8), 8), LANES:]
            moved = pltpu.roll(jnp.where(lane == 0, after, cross), LANES - 1, 1)
            other = pltpu.roll(jnp.where(sublane < 4, moved, cross), 4, 0)
            out_ref[0, y, z, c, x] = (same + other).astype(BF16)
            out_ref[1, y, z, c, x] = (same - other).astype(BF16)
        return carry

    lax.fori_loop(0, blocks // c_count, finish, 0, unroll=4)


def filtered(signal, taps, sizes):
    s, yl, x, z, c = sizes
    blocks = signal.shape[0]
    depth = SHIFTS * LANES
    return pl.pallas_call(
        filter_kernel,
        grid=(1,),
        out_shape=jax.ShapeDtypeStruct((s, yl, z, c, x, 8, LANES), BF16),
        in_specs=[VMEM, ANY],
        out_specs=VMEM,
        scratch_shapes=[
            pltpu.VMEM(((blocks + SHIFTS) * 8, LANES), F32),
            pltpu.VMEM((blocks * 8, depth), BF16),
            pltpu.VMEM((blocks * 8 + 8, 2 * LANES), F32),
            pltpu.VMEM(taps.shape, BF16),
            pltpu.SemaphoreType.DMA((blocks // SHIFTS,)),
        ],
        compiler_params=pltpu.CompilerParams(vmem_limit_bytes=52 << 20),
        cost_estimate=pl.CostEstimate(
            flops=blocks * 8 * depth * blocks * LANES * 8 // 8,
            bytes_accessed=taps.shape[0] * taps.shape[1] * 2,
            transcendentals=0,
        ),
    )(signal, taps)


def along(array, axis, size, offset):
    return lax.ppermute(array, axis, [(i, (i + offset) % size) for i in range(size)])


def turn_kernel(order_ref, cotangent_ref, out_ref, turned):
    turned[...] = lax.dot_general(
        cotangent_ref[...], order_ref[...], (((0,), (0,)), ((), ())), preferred_element_type=F32
    )
    sign = lax.axis_index("s")
    upper = lax.broadcasted_iota(jnp.int32, (8, LANES), 0) < 4

    def place(i, carry):
        row = pl.multiple_of(i * 8, 8)
        even, odd = turned[pl.ds(row, 8), :LANES], turned[pl.ds(row, 8), LANES:]
        lower_rows = jnp.where(upper, even, pltpu.roll(odd, 4, 0))
        upper_rows = jnp.where(upper, pltpu.roll(even, 4, 0), odd)
        out_ref[i] = jnp.where(sign == 0, lower_rows, upper_rows).astype(BF16)
        return carry

    lax.fori_loop(0, out_ref.shape[0], place, 0, unroll=8)


def turn(order, cotangent):
    tokens, width = cotangent.shape
    return pl.pallas_call(
        turn_kernel,
        out_shape=jax.ShapeDtypeStruct((width // 8, 8, tokens // 2), BF16),
        in_specs=[VMEM, VMEM],
        out_specs=VMEM,
        scratch_shapes=[pltpu.VMEM((width, tokens), F32)],
        compiler_params=pltpu.CompilerParams(vmem_limit_bytes=16 << 20),
    )(order, cotangent)


def pair(first, second, upper):
    first, second = first.astype(F32), second.astype(F32)
    even = jnp.where(upper, first, pltpu.roll(second, 4, 0))
    odd = jnp.where(upper, pltpu.roll(first, 4, 0), second)
    return even.astype(BF16), odd.astype(BF16)


def arrange_kernel(order_ref, *refs):
    *gathered, out_ref, held, arrived = refs
    tokens = order_ref.shape[0]
    copies, row = [], 0
    for n, ref in enumerate(gathered):
        copies.append(
            pltpu.make_async_copy(ref, held.at[row : row + ref.shape[0], :], arrived.at[n])
        )
        row += ref.shape[0]
        copies[n].start()
    for copy in copies:
        copy.wait()
    for k in range(row // tokens):
        part = slice(k * tokens, (k + 1) * tokens)
        out_ref[part, :] = lax.dot_general(
            order_ref[...], held[part, :], (((0,), (0,)), ((), ())), preferred_element_type=F32
        ).astype(BF16)


def arrange(order, gathered):
    rows, width = sum(part.shape[0] for part in gathered), gathered[0].shape[1]
    return pl.pallas_call(
        arrange_kernel,
        out_shape=jax.ShapeDtypeStruct((rows, width), BF16),
        in_specs=[VMEM] + [ANY] * len(gathered),
        out_specs=VMEM,
        scratch_shapes=[
            pltpu.VMEM((rows, width), BF16),
            pltpu.SemaphoreType.DMA((len(gathered),)),
        ],
        compiler_params=pltpu.CompilerParams(vmem_limit_bytes=24 << 20),
        cost_estimate=pl.CostEstimate(
            flops=2 * rows * order.shape[0] * width,
            bytes_accessed=4 * rows * width,
            transcendentals=0,
        ),
    )(order, *gathered)


def weight_kernel(spread_ref, inputs_ref, own_ref, other_ref, left):
    x = spread_ref.shape[1]
    half = spread_ref.shape[0] // 2
    tiles = half // 2
    x_here, c_here = lax.axis_index("x"), lax.axis_index("c")
    upper = lax.broadcasted_iota(jnp.int32, (8, LANES), 0) < 4
    for k in range(x):
        block = lax.rem(x_here - k + x, x)
        for part in range(2):
            core = c_here if part == 0 else 1 - c_here

            def place(i, carry, k=k, block=block, part=part, core=core):
                pairs = [
                    pair(
                        spread_ref[2 * (2 * i + n) + core, block],
                        spread_ref[half + 2 * (2 * i + n) + core, block],
                        upper,
                    )
                    for n in range(2)
                ]
                at = pl.multiple_of(part * tiles * 8 + i * 16, 16)
                for parity in range(2):
                    col = (2 * k + parity) * LANES
                    left[pl.ds(at, 16), col : col + LANES] = jnp.concatenate(
                        [pairs[0][parity], pairs[1][parity]], 0
                    )
                return carry

            lax.fori_loop(0, tiles // 2, place, 0, unroll=4)
    y = jnp.dot(left[...], inputs_ref[...], preferred_element_type=F32).astype(BF16)
    own_ref[...] = y[: tiles * 8, :]
    other_ref[...] = y[tiles * 8 :, :]


def weight_part(spread, arranged):
    count = spread.shape[0]
    depth, width = arranged.shape
    rows = count * 4
    return pl.pallas_call(
        weight_kernel,
        out_shape=[jax.ShapeDtypeStruct((rows // 2, width), BF16)] * 2,
        in_specs=[VMEM, VMEM],
        out_specs=[VMEM, VMEM],
        scratch_shapes=[pltpu.VMEM((rows, depth), BF16)],
        compiler_params=pltpu.CompilerParams(vmem_limit_bytes=24 << 20),
        cost_estimate=pl.CostEstimate(
            flops=2 * rows * depth * width,
            bytes_accessed=4 * depth * width,
            transcendentals=0,
        ),
    )(spread, arranged)


def project_kernel(order_ref, weights_ref, *refs):
    *home, mine_ref, theirs_ref, columns, part, matrix, arrived = refs
    copy = pltpu.make_async_copy(weights_ref, matrix, arrived)
    copy.start()
    x = len(home)
    half = home[0].shape[0] // 2
    width = weights_ref.shape[0]
    yl = width // (LANES * x)
    x_here, sign = lax.axis_index("x"), lax.axis_index("s")
    upper = lax.broadcasted_iota(jnp.int32, (8, LANES), 0) < 4
    per = half // yl
    for k in range(x):
        block = lax.rem(x_here - k + x, x)
        for y in range(yl):

            def place(i, carry, k=k, y=y, block=block):
                q = y * per + 2 * i
                tile_pairs = [
                    pair(home[k][q + n], home[k][half + q + n], upper) for n in range(2)
                ]
                row = pl.multiple_of((y * x + block) * LANES + i * 16, 16)
                for parity in range(2):
                    columns[pl.ds(row, 16), parity * LANES : (parity + 1) * LANES] = (
                        jnp.concatenate([tile_pairs[0][parity], tile_pairs[1][parity]], 0)
                    )
                return carry

            lax.fori_loop(0, per // 2, place, 0, unroll=4)
    copy.wait()
    part[...] = lax.dot_general(
        columns[...], matrix[...], (((0,), (0,)), ((), ())), preferred_element_type=F32
    ).astype(BF16)
    whole = jnp.dot(order_ref[...], part[...], preferred_element_type=F32).astype(BF16)
    side = width // 2

    @pl.when(sign == 0)
    def _():
        mine_ref[...] = whole[:, :side]
        theirs_ref[...] = whole[:, side:]

    @pl.when(sign == 1)
    def _():
        mine_ref[...] = whole[:, side:]
        theirs_ref[...] = whole[:, :side]


def project(order, weights, home):
    tokens, width = order.shape[0], weights.shape[0]
    return pl.pallas_call(
        project_kernel,
        out_shape=[jax.ShapeDtypeStruct((tokens, width // 2), BF16)] * 2,
        in_specs=[VMEM, ANY] + [VMEM] * len(home),
        out_specs=[VMEM, VMEM],
        scratch_shapes=[
            pltpu.VMEM((width, tokens), BF16),
            pltpu.VMEM((tokens, width), BF16),
            pltpu.VMEM((width, width), BF16),
            pltpu.SemaphoreType.DMA,
        ],
        compiler_params=pltpu.CompilerParams(vmem_limit_bytes=24 << 20),
        cost_estimate=pl.CostEstimate(
            flops=2 * tokens * width * width, bytes_accessed=4 * width * width, transcendentals=0
        ),
    )(order, weights, *home)


def body(inputs, cotangent, weights, filter_taps):
    sizes = SIZES
    s, yl, x, z, c = sizes
    tokens, width = inputs.shape
    half = tokens // 2
    groups = yl * x * z * c
    x_here = lax.axis_index("x")
    row = lax.broadcasted_iota(jnp.int32, (tokens, tokens), 0)
    col = lax.broadcasted_iota(jnp.int32, (tokens, tokens), 1)
    order = (row == 2 * (col % half) + col // half).astype(BF16)

    send = turn(order, cotangent)
    signal = lax.all_to_all(send, ("yl", "x", "z", "c"), split_axis=0, concat_axis=0, tiled=True)

    taps = toeplitz(filter_taps)
    taps, inputs = lax.optimization_barrier((taps, inputs))
    before, after = along(inputs, "x", x, 1), along(inputs, "x", x, x - 1)

    result = filtered(signal, taps, sizes).reshape(s * yl * z * c, x, 8, half)
    result, before, after = lax.optimization_barrier((result, before, after))
    gathered = [
        inputs,
        before,
        along(before[:half], "x", x, 1),
        along(after[half:], "x", x, x - 1),
        after,
    ]
    spread = lax.all_to_all(result, ("s", "yl", "z", "c"), split_axis=0, concat_axis=0, tiled=True)
    home = [
        lax.dynamic_index_in_dim(spread, lax.rem(x_here + k, x), 1, keepdims=False)
        for k in range(x)
    ]

    own, other = weight_part(spread, arrange(order, gathered))
    other, *home = lax.optimization_barrier((other, *home))
    home = [home[0]] + [along(home[k], "x", x, k) for k in range(1, x)]
    other = along(other, "c", c, 1)
    reduced = (own.astype(F32) + other.astype(F32)).astype(BF16).reshape(yl * z, 8, width)
    _, *home = lax.optimization_barrier((reduced, *home))
    mine, theirs = project(order, weights[0], home)
    arrived = jnp.concatenate([along(theirs[:half], "s", s, 1), along(theirs[half:], "s", s, 1)])
    pieces = lax.all_to_all(reduced, ("yl", "z"), split_axis=0, concat_axis=0, tiled=True)
    grad_scale = 1.0 / math.sqrt(tokens * groups)
    weight_grad = jnp.sum(pieces.astype(F32), 0) * grad_scale
    input_grad = (mine.astype(F32) + arrived.astype(F32)).astype(BF16)
    return input_grad, weight_grad[None]


def solution(mesh):
    fine = Mesh(mesh.devices.reshape(SIZES), AXES)
    context = ("yl", "x", "z", "c")
    in_specs = (P(context, None), P(context, None), P("s", None, None), P())
    out_specs = (P(context, "s"), P("s", context, None))
    return jax.shard_map(body, mesh=fine, in_specs=in_specs, out_specs=out_specs, check_vma=False)
```

```python
import functools
import math

import jax
import jax.numpy as jnp
from jax import lax
from jax.experimental import pallas as pl
from jax.experimental.pallas import tpu as pltpu
from jax.sharding import Mesh, PartitionSpec as P

BF16, F32 = jnp.bfloat16, jnp.float32
LANES = 128
AXES = ("s", "yl", "x", "z", "c")
SIZES = (2, 2, 4, 8, 2)
VMEM = pl.BlockSpec(memory_space=pltpu.VMEM)
ANY = pl.BlockSpec(memory_space=pl.ANY)


def toeplitz_kernel(taps_ref, out_ref, rows):
    blocks = out_ref.shape[0] // LANES
    source = lax.broadcasted_iota(jnp.int32, (2 * LANES, 2 * LANES), 0)
    target = lax.broadcasted_iota(jnp.int32, (2 * LANES, 2 * LANES), 1)
    select = source == 2 * (LANES - 1 - target % LANES) + target // LANES

    @pl.when(pl.program_id(0) == 0)
    def _():
        chosen = sum(
            jnp.dot(
                taps_ref[pl.ds(n, taps_ref.shape[0] // 2, stride=2), :],
                select[n * LANES : (n + 1) * LANES].astype(F32),
                precision=lax.Precision.HIGHEST,
                preferred_element_type=F32,
            )
            for n in range(2)
        )
        for parity in range(2):
            rows[parity, 0:8, :] = jnp.zeros((8, LANES), F32)
            rows[parity, 8:, :] = chosen[:, parity * LANES : (parity + 1) * LANES]

    keep = lax.broadcasted_iota(jnp.int32, (LANES, LANES), 1) < LANES - 1 - lax.broadcasted_iota(
        jnp.int32, (LANES, LANES), 0
    )
    first = pl.program_id(0) * blocks

    def body(m, carry):
        row = pl.multiple_of(m * LANES, LANES)
        for parity in range(2):
            before = jnp.broadcast_to(rows[parity, pl.ds(first + m + 7, 1), :], (LANES, LANES))
            here = jnp.broadcast_to(rows[parity, pl.ds(first + m + 8, 1), :], (LANES, LANES))
            tile = pltpu.roll(jnp.where(keep, before, here), 1, 1, stride=1, stride_axis=0)
            high = tile.astype(BF16)
            out_ref[pl.ds(row, LANES), parity * LANES : (parity + 1) * LANES] = high
            out_ref[pl.ds(row, LANES), (2 + parity) * LANES : (3 + parity) * LANES] = (
                tile - high.astype(F32)
            ).astype(BF16)
        return carry

    lax.fori_loop(0, blocks, body, 0, unroll=8)


def toeplitz(filter_taps):
    count = filter_taps.shape[0] // 2
    parts = 4
    return pl.pallas_call(
        toeplitz_kernel,
        grid=(parts,),
        out_shape=jax.ShapeDtypeStruct((count, 4 * LANES), BF16),
        in_specs=[pl.BlockSpec((2 * count // LANES, LANES), lambda i: (0, 0))],
        out_specs=pl.BlockSpec((count // parts, 4 * LANES), lambda i: (i, 0)),
        scratch_shapes=[pltpu.VMEM((2, count // LANES + 8, LANES), F32)],
        compiler_params=pltpu.CompilerParams(vmem_limit_bytes=52 << 20),
        cost_estimate=pl.CostEstimate(
            flops=count * 2048, bytes_accessed=count * 1024, transcendentals=0
        ),
    )(filter_taps.reshape(2 * count // LANES, LANES))


SHIFTS = 16
GROUPS = 8


def filter_kernel(signal_ref, taps_ref, out_ref, held, left, total, table, arrived):
    blocks = signal_ref.shape[0]
    rows = blocks * 8
    steps = blocks // SHIFTS
    per = steps // GROUPS
    depth = SHIFTS * LANES

    def fetch(step):
        part = pl.ds(pl.multiple_of(step * depth, depth), depth)
        return pltpu.make_async_copy(taps_ref.at[part, :], table.at[part, :], arrived.at[step])

    def start(step, carry):
        fetch(step).start()
        return carry

    lax.fori_loop(0, steps, start, 0)

    held[:rows, :] = signal_ref[...].astype(F32).reshape(rows, LANES)
    held[rows:, :] = jnp.zeros((SHIFTS * 8, LANES), F32)

    def fill(i, carry):
        row = pl.multiple_of(i * LANES, LANES)
        for d in range(SHIFTS):
            left[pl.ds(row, LANES), d * LANES : (d + 1) * LANES] = held[
                pl.ds(pl.multiple_of(row + 8 * d, 8), LANES), :
            ].astype(BF16)
        total[pl.ds(row, LANES), :] = jnp.zeros((LANES, 2 * LANES), F32)
        return carry

    lax.fori_loop(0, rows // LANES, fill, 0)
    total[rows:, :] = jnp.zeros((8, 2 * LANES), F32)
    for g in range(GROUPS):
        count = rows - g * per * SHIFTS * 8

        def multiply(j, carry, g=g, count=count):
            step = g * per + j
            fetch(step).wait()
            a = left[pl.ds(pl.multiple_of(step * SHIFTS * 8, SHIFTS * 8), count), :]
            t = table[pl.ds(pl.multiple_of(step * depth, depth), depth), :]
            y = jnp.dot(a, t, preferred_element_type=F32)
            total[0:count, :] += y[:, : 2 * LANES] + y[:, 2 * LANES :]
            return carry

        lax.fori_loop(0, per * (1 + pl.program_id(0)), multiply, 0)

    lane = lax.broadcasted_iota(jnp.int32, (8, LANES), 1)
    sublane = lax.broadcasted_iota(jnp.int32, (8, LANES), 0)
    _, y_count, z_count, c_count, x_count = out_ref.shape[:5]

    def finish(i, carry):
        yx, z = i // z_count, i % z_count
        y, x = yx // x_count, yx % x_count
        for c in range(c_count):
            row = pl.multiple_of((i * c_count + c) * 8, 8)
            same = total[pl.ds(row, 8), :LANES]
            cross = total[pl.ds(row, 8), LANES:]
            after = total[pl.ds(pl.multiple_of(row + 8, 8), 8), LANES:]
            moved = pltpu.roll(jnp.where(lane == 0, after, cross), LANES - 1, 1)
            other = pltpu.roll(jnp.where(sublane < 4, moved, cross), 4, 0)
            out_ref[0, y, z, c, x] = (same + other).astype(BF16)
            out_ref[1, y, z, c, x] = (same - other).astype(BF16)
        return carry

    lax.fori_loop(0, blocks // c_count, finish, 0, unroll=8)


def filtered(signal, taps, sizes):
    s, yl, x, z, c = sizes
    blocks = signal.shape[0]
    depth = SHIFTS * LANES
    return pl.pallas_call(
        filter_kernel,
        grid=(1,),
        out_shape=jax.ShapeDtypeStruct((s, yl, z, c, x, 8, LANES), BF16),
        in_specs=[VMEM, ANY],
        out_specs=VMEM,
        scratch_shapes=[
            pltpu.VMEM(((blocks + SHIFTS) * 8, LANES), F32),
            pltpu.VMEM((blocks * 8, depth), BF16),
            pltpu.VMEM((blocks * 8 + 8, 2 * LANES), F32),
            pltpu.VMEM(taps.shape, BF16),
            pltpu.SemaphoreType.DMA((blocks // SHIFTS,)),
        ],
        compiler_params=pltpu.CompilerParams(vmem_limit_bytes=52 << 20),
        cost_estimate=pl.CostEstimate(
            flops=blocks * 8 * depth * blocks * LANES * 8 // 8,
            bytes_accessed=taps.shape[0] * taps.shape[1] * 2,
            transcendentals=0,
        ),
    )(signal, taps)


def along(array, axis, size, offset):
    return lax.ppermute(array, axis, [(i, (i + offset) % size) for i in range(size)])


def turn_kernel(order_ref, cotangent_ref, out_ref, turned):
    turned[...] = lax.dot_general(
        cotangent_ref[...], order_ref[...], (((0,), (0,)), ((), ())), preferred_element_type=F32
    )
    sign = lax.axis_index("s")
    upper = lax.broadcasted_iota(jnp.int32, (8, LANES), 0) < 4

    def place(i, carry):
        row = pl.multiple_of(i * 8, 8)
        even, odd = turned[pl.ds(row, 8), :LANES], turned[pl.ds(row, 8), LANES:]
        lower_rows = jnp.where(upper, even, pltpu.roll(odd, 4, 0))
        upper_rows = jnp.where(upper, pltpu.roll(even, 4, 0), odd)
        out_ref[i] = jnp.where(sign == 0, lower_rows, upper_rows).astype(BF16)
        return carry

    lax.fori_loop(0, out_ref.shape[0], place, 0, unroll=8)


def turn(order, cotangent):
    tokens, width = cotangent.shape
    return pl.pallas_call(
        turn_kernel,
        out_shape=jax.ShapeDtypeStruct((width // 8, 8, tokens // 2), BF16),
        in_specs=[VMEM, VMEM],
        out_specs=VMEM,
        scratch_shapes=[pltpu.VMEM((width, tokens), F32)],
        compiler_params=pltpu.CompilerParams(vmem_limit_bytes=16 << 20),
    )(order, cotangent)


def pair(first, second, upper):
    first, second = first.astype(F32), second.astype(F32)
    even = jnp.where(upper, first, pltpu.roll(second, 4, 0))
    odd = jnp.where(upper, pltpu.roll(first, 4, 0), second)
    return even.astype(BF16), odd.astype(BF16)


def arrange_kernel(order_ref, *refs):
    *gathered, out_ref, held, arrived = refs
    tokens = order_ref.shape[0]
    copies, row = [], 0
    for n, ref in enumerate(gathered):
        copies.append(
            pltpu.make_async_copy(ref, held.at[row : row + ref.shape[0], :], arrived.at[n])
        )
        row += ref.shape[0]
        copies[n].start()
    for copy in copies:
        copy.wait()
    for k in range(row // tokens):
        part = slice(k * tokens, (k + 1) * tokens)
        out_ref[part, :] = lax.dot_general(
            order_ref[...], held[part, :], (((0,), (0,)), ((), ())), preferred_element_type=F32
        ).astype(BF16)


def arrange(order, gathered):
    rows, width = sum(part.shape[0] for part in gathered), gathered[0].shape[1]
    return pl.pallas_call(
        arrange_kernel,
        out_shape=jax.ShapeDtypeStruct((rows, width), BF16),
        in_specs=[VMEM] + [ANY] * len(gathered),
        out_specs=VMEM,
        scratch_shapes=[
            pltpu.VMEM((rows, width), BF16),
            pltpu.SemaphoreType.DMA((len(gathered),)),
        ],
        compiler_params=pltpu.CompilerParams(vmem_limit_bytes=24 << 20),
        cost_estimate=pl.CostEstimate(
            flops=2 * rows * order.shape[0] * width,
            bytes_accessed=4 * rows * width,
            transcendentals=0,
        ),
    )(order, *gathered)


def weight_kernel(scale, spread_ref, inputs_ref, own_ref, other_ref, left):
    x = spread_ref.shape[1]
    half = spread_ref.shape[0] // 2
    tiles = half // 2
    x_here, c_here = lax.axis_index("x"), lax.axis_index("c")
    upper = lax.broadcasted_iota(jnp.int32, (8, LANES), 0) < 4
    for k in range(x):
        block = lax.rem(x_here - k + x, x)
        for part in range(2):
            core = c_here if part == 0 else 1 - c_here

            def place(i, carry, k=k, block=block, part=part, core=core):
                pairs = [
                    pair(
                        spread_ref[2 * (2 * i + n) + core, block],
                        spread_ref[half + 2 * (2 * i + n) + core, block],
                        upper,
                    )
                    for n in range(2)
                ]
                at = pl.multiple_of(part * tiles * 8 + i * 16, 16)
                for parity in range(2):
                    col = (2 * k + parity) * LANES
                    left[pl.ds(at, 16), col : col + LANES] = jnp.concatenate(
                        [pairs[0][parity], pairs[1][parity]], 0
                    )
                return carry

            lax.fori_loop(0, tiles // 2, place, 0, unroll=4)
    y = (jnp.dot(left[...], inputs_ref[...], preferred_element_type=F32) * scale).astype(BF16)
    own_ref[...] = y[: tiles * 8, :]
    other_ref[...] = y[tiles * 8 :, :]


def weight_part(spread, arranged, scale):
    count = spread.shape[0]
    depth, width = arranged.shape
    rows = count * 4
    return pl.pallas_call(
        functools.partial(weight_kernel, scale),
        out_shape=[jax.ShapeDtypeStruct((rows // 2, width), BF16)] * 2,
        in_specs=[VMEM, VMEM],
        out_specs=[VMEM, VMEM],
        scratch_shapes=[pltpu.VMEM((rows, depth), BF16)],
        compiler_params=pltpu.CompilerParams(vmem_limit_bytes=24 << 20),
        cost_estimate=pl.CostEstimate(
            flops=2 * rows * depth * width,
            bytes_accessed=4 * depth * width,
            transcendentals=0,
        ),
    )(spread, arranged)


def project_kernel(order_ref, weights_ref, *refs):
    *home, mine_ref, theirs_ref, columns, part, matrix, arrived = refs
    copy = pltpu.make_async_copy(weights_ref, matrix, arrived)
    copy.start()
    x = len(home)
    half = home[0].shape[0] // 2
    width = weights_ref.shape[0]
    yl = width // (LANES * x)
    x_here, sign = lax.axis_index("x"), lax.axis_index("s")
    upper = lax.broadcasted_iota(jnp.int32, (8, LANES), 0) < 4
    per = half // yl
    for k in range(x):
        block = lax.rem(x_here - k + x, x)
        for y in range(yl):

            def place(i, carry, k=k, y=y, block=block):
                q = y * per + 2 * i
                tile_pairs = [
                    pair(home[k][q + n], home[k][half + q + n], upper) for n in range(2)
                ]
                row = pl.multiple_of((y * x + block) * LANES + i * 16, 16)
                for parity in range(2):
                    columns[pl.ds(row, 16), parity * LANES : (parity + 1) * LANES] = (
                        jnp.concatenate([tile_pairs[0][parity], tile_pairs[1][parity]], 0)
                    )
                return carry

            lax.fori_loop(0, per // 2, place, 0, unroll=4)
    copy.wait()
    part[...] = lax.dot_general(
        columns[...], matrix[...], (((0,), (0,)), ((), ())), preferred_element_type=F32
    ).astype(BF16)
    whole = jnp.dot(order_ref[...], part[...], preferred_element_type=F32).astype(BF16)
    side = width // 2

    @pl.when(sign == 0)
    def _():
        mine_ref[...] = whole[:, :side]
        theirs_ref[...] = whole[:, side:]

    @pl.when(sign == 1)
    def _():
        mine_ref[...] = whole[:, side:]
        theirs_ref[...] = whole[:, :side]


def project(order, weights, home):
    tokens, width = order.shape[0], weights.shape[0]
    return pl.pallas_call(
        project_kernel,
        out_shape=[jax.ShapeDtypeStruct((tokens, width // 2), BF16)] * 2,
        in_specs=[VMEM, ANY] + [VMEM] * len(home),
        out_specs=[VMEM, VMEM],
        scratch_shapes=[
            pltpu.VMEM((width, tokens), BF16),
            pltpu.VMEM((tokens, width), BF16),
            pltpu.VMEM((width, width), BF16),
            pltpu.SemaphoreType.DMA,
        ],
        compiler_params=pltpu.CompilerParams(vmem_limit_bytes=24 << 20),
        cost_estimate=pl.CostEstimate(
            flops=2 * tokens * width * width, bytes_accessed=4 * width * width, transcendentals=0
        ),
    )(order, weights, *home)


def body(inputs, cotangent, weights, filter_taps):
    sizes = SIZES
    s, yl, x, z, c = sizes
    tokens, width = inputs.shape
    half = tokens // 2
    groups = yl * x * z * c
    x_here = lax.axis_index("x")
    row = lax.broadcasted_iota(jnp.int32, (tokens, tokens), 0)
    col = lax.broadcasted_iota(jnp.int32, (tokens, tokens), 1)
    order = (row == 2 * (col % half) + col // half).astype(BF16)

    send = turn(order, cotangent)
    signal = lax.all_to_all(send, ("yl", "x", "z", "c"), split_axis=0, concat_axis=0, tiled=True)

    taps = toeplitz(filter_taps)
    taps, inputs = lax.optimization_barrier((taps, inputs))
    before, after = along(inputs, "x", x, 1), along(inputs, "x", x, x - 1)

    result = filtered(signal, taps, sizes).reshape(s * yl * z * c, x, 8, half)
    result, before, after = lax.optimization_barrier((result, before, after))
    gathered = [
        inputs,
        before,
        along(before[:half], "x", x, 1),
        along(after[half:], "x", x, x - 1),
        after,
    ]
    spread = lax.all_to_all(result, ("s", "yl", "z", "c"), split_axis=0, concat_axis=0, tiled=True)
    home = [
        lax.dynamic_index_in_dim(spread, lax.rem(x_here + k, x), 1, keepdims=False)
        for k in range(x)
    ]

    grad_scale = 1.0 / math.sqrt(tokens * groups)
    own, other = weight_part(spread, arrange(order, gathered), grad_scale)
    other, *home = lax.optimization_barrier((other, *home))
    home = [home[0]] + [along(home[k], "x", x, k) for k in range(1, x)]
    other = along(other, "c", c, 1)
    reduced = (own.astype(F32) + other.astype(F32)).astype(BF16).reshape(yl * z, 8, width)
    _, *home = lax.optimization_barrier((reduced, *home))
    mine, theirs = project(order, weights[0], home)
    arrived = jnp.concatenate([along(theirs[:half], "s", s, 1), along(theirs[half:], "s", s, 1)])
    pieces = lax.all_to_all(reduced, ("yl", "z"), split_axis=0, concat_axis=0, tiled=True)
    weight_grad = jnp.sum(pieces.astype(F32), 0)
    input_grad = (mine.astype(F32) + arrived.astype(F32)).astype(BF16)
    return input_grad, weight_grad[None]


def solution(mesh):
    fine = Mesh(mesh.devices.reshape(SIZES), AXES)
    context = ("yl", "x", "z", "c")
    in_specs = (P(context, None), P(context, None), P("s", None, None), P())
    out_specs = (P(context, "s"), P("s", context, None))
    return jax.shard_map(body, mesh=fine, in_specs=in_specs, out_specs=out_specs, check_vma=False)
```

```python
import functools
import math

import jax
import jax.numpy as jnp
from jax import lax
from jax.experimental import pallas as pl
from jax.experimental.pallas import tpu as pltpu
from jax.sharding import Mesh, PartitionSpec as P

BF16, F32 = jnp.bfloat16, jnp.float32
LANES = 128
AXES = ("s", "yl", "x", "z", "c")
SIZES = (2, 2, 4, 8, 2)
VMEM = pl.BlockSpec(memory_space=pltpu.VMEM)
ANY = pl.BlockSpec(memory_space=pl.ANY)


def toeplitz_kernel(taps_ref, out_ref, rows):
    blocks = out_ref.shape[0] // LANES
    source = lax.broadcasted_iota(jnp.int32, (2 * LANES, 2 * LANES), 0)
    target = lax.broadcasted_iota(jnp.int32, (2 * LANES, 2 * LANES), 1)
    select = source == 2 * (LANES - 1 - target % LANES) + target // LANES

    @pl.when(pl.program_id(0) == 0)
    def _():
        chosen = sum(
            jnp.dot(
                taps_ref[pl.ds(n, taps_ref.shape[0] // 2, stride=2), :],
                select[n * LANES : (n + 1) * LANES].astype(F32),
                precision=lax.Precision.HIGHEST,
                preferred_element_type=F32,
            )
            for n in range(2)
        )
        for parity in range(2):
            rows[parity, 0:8, :] = jnp.zeros((8, LANES), F32)
            rows[parity, 8:, :] = chosen[:, parity * LANES : (parity + 1) * LANES]

    keep = lax.broadcasted_iota(jnp.int32, (LANES, LANES), 1) < LANES - 1 - lax.broadcasted_iota(
        jnp.int32, (LANES, LANES), 0
    )
    first = pl.program_id(0) * blocks

    def body(m, carry):
        row = pl.multiple_of(m * LANES, LANES)
        for parity in range(2):
            before = jnp.broadcast_to(rows[parity, pl.ds(first + m + 7, 1), :], (LANES, LANES))
            here = jnp.broadcast_to(rows[parity, pl.ds(first + m + 8, 1), :], (LANES, LANES))
            tile = pltpu.roll(jnp.where(keep, before, here), 1, 1, stride=1, stride_axis=0)
            high = tile.astype(BF16)
            out_ref[pl.ds(row, LANES), parity * LANES : (parity + 1) * LANES] = high
            out_ref[pl.ds(row, LANES), (2 + parity) * LANES : (3 + parity) * LANES] = (
                tile - high.astype(F32)
            ).astype(BF16)
        return carry

    lax.fori_loop(0, blocks, body, 0, unroll=8)


def toeplitz(filter_taps):
    count = filter_taps.shape[0] // 2
    parts = 4
    return pl.pallas_call(
        toeplitz_kernel,
        grid=(parts,),
        out_shape=jax.ShapeDtypeStruct((count, 4 * LANES), BF16),
        in_specs=[pl.BlockSpec((2 * count // LANES, LANES), lambda i: (0, 0))],
        out_specs=pl.BlockSpec((count // parts, 4 * LANES), lambda i: (i, 0)),
        scratch_shapes=[pltpu.VMEM((2, count // LANES + 8, LANES), F32)],
        compiler_params=pltpu.CompilerParams(vmem_limit_bytes=52 << 20),
        cost_estimate=pl.CostEstimate(
            flops=count * 2048, bytes_accessed=count * 1024, transcendentals=0
        ),
    )(filter_taps.reshape(2 * count // LANES, LANES))


SHIFTS = 16
GROUPS = 8


def filter_kernel(signal_ref, taps_ref, out_ref, held, left, total, table, arrived):
    blocks = signal_ref.shape[0]
    rows = blocks * 8
    steps = blocks // SHIFTS
    per = steps // GROUPS
    depth = SHIFTS * LANES

    def fetch(step):
        part = pl.ds(pl.multiple_of(step * depth, depth), depth)
        return pltpu.make_async_copy(taps_ref.at[part, :], table.at[part, :], arrived.at[step])

    def start(step, carry):
        fetch(step).start()
        return carry

    lax.fori_loop(0, steps, start, 0)

    held[:rows, :] = signal_ref[...].astype(F32).reshape(rows, LANES)
    held[rows:, :] = jnp.zeros((SHIFTS * 8, LANES), F32)

    def fill(i, carry):
        row = pl.multiple_of(i * LANES, LANES)
        for d in range(SHIFTS):
            left[pl.ds(row, LANES), d * LANES : (d + 1) * LANES] = held[
                pl.ds(pl.multiple_of(row + 8 * d, 8), LANES), :
            ].astype(BF16)
        total[pl.ds(row, LANES), :] = jnp.zeros((LANES, 2 * LANES), F32)
        return carry

    lax.fori_loop(0, rows // LANES, fill, 0)
    total[rows:, :] = jnp.zeros((8, 2 * LANES), F32)
    for g in range(GROUPS):
        count = rows - g * per * SHIFTS * 8

        def multiply(j, carry, g=g, count=count):
            step = g * per + j
            fetch(step).wait()
            a = left[pl.ds(pl.multiple_of(step * SHIFTS * 8, SHIFTS * 8), count), :]
            t = table[pl.ds(pl.multiple_of(step * depth, depth), depth), :]
            y = jnp.dot(a, t, preferred_element_type=F32)
            total[0:count, :] += y[:, : 2 * LANES] + y[:, 2 * LANES :]
            return carry

        lax.fori_loop(0, per * (1 + pl.program_id(0)), multiply, 0)

    lane = lax.broadcasted_iota(jnp.int32, (8, LANES), 1)
    sublane = lax.broadcasted_iota(jnp.int32, (8, LANES), 0)
    _, y_count, z_count, c_count, x_count = out_ref.shape[:5]

    def finish(i, carry):
        yx, z = i // z_count, i % z_count
        y, x = yx // x_count, yx % x_count
        for c in range(c_count):
            row = pl.multiple_of((i * c_count + c) * 8, 8)
            same = total[pl.ds(row, 8), :LANES]
            cross = total[pl.ds(row, 8), LANES:]
            after = total[pl.ds(pl.multiple_of(row + 8, 8), 8), LANES:]
            moved = pltpu.roll(jnp.where(lane == 0, after, cross), LANES - 1, 1)
            other = pltpu.roll(jnp.where(sublane < 4, moved, cross), 4, 0)
            out_ref[0, y, z, c, x] = (same + other).astype(BF16)
            out_ref[1, y, z, c, x] = (same - other).astype(BF16)
        return carry

    lax.fori_loop(0, blocks // c_count, finish, 0, unroll=8)


def filtered(signal, taps, sizes):
    s, yl, x, z, c = sizes
    blocks = signal.shape[0]
    depth = SHIFTS * LANES
    return pl.pallas_call(
        filter_kernel,
        grid=(1,),
        out_shape=jax.ShapeDtypeStruct((s, yl, z, c, x, 8, LANES), BF16),
        in_specs=[VMEM, ANY],
        out_specs=VMEM,
        scratch_shapes=[
            pltpu.VMEM(((blocks + SHIFTS) * 8, LANES), F32),
            pltpu.VMEM((blocks * 8, depth), BF16),
            pltpu.VMEM((blocks * 8 + 8, 2 * LANES), F32),
            pltpu.VMEM(taps.shape, BF16),
            pltpu.SemaphoreType.DMA((blocks // SHIFTS,)),
        ],
        compiler_params=pltpu.CompilerParams(vmem_limit_bytes=52 << 20),
        cost_estimate=pl.CostEstimate(
            flops=blocks * 8 * depth * blocks * LANES * 8 // 8,
            bytes_accessed=taps.shape[0] * taps.shape[1] * 2,
            transcendentals=0,
        ),
    )(signal, taps)


def along(array, axis, size, offset):
    return lax.ppermute(array, axis, [(i, (i + offset) % size) for i in range(size)])


def turn_kernel(order_ref, cotangent_ref, out_ref, turned):
    turned[...] = lax.dot_general(
        cotangent_ref[...], order_ref[...], (((0,), (0,)), ((), ())), preferred_element_type=F32
    )
    sign = lax.axis_index("s")
    upper = lax.broadcasted_iota(jnp.int32, (8, LANES), 0) < 4

    def place(i, carry):
        row = pl.multiple_of(i * 8, 8)
        even, odd = turned[pl.ds(row, 8), :LANES], turned[pl.ds(row, 8), LANES:]
        lower_rows = jnp.where(upper, even, pltpu.roll(odd, 4, 0))
        upper_rows = jnp.where(upper, pltpu.roll(even, 4, 0), odd)
        out_ref[i] = jnp.where(sign == 0, lower_rows, upper_rows).astype(BF16)
        return carry

    lax.fori_loop(0, out_ref.shape[0], place, 0, unroll=8)


def turn(order, cotangent):
    tokens, width = cotangent.shape
    return pl.pallas_call(
        turn_kernel,
        out_shape=jax.ShapeDtypeStruct((width // 8, 8, tokens // 2), BF16),
        in_specs=[VMEM, VMEM],
        out_specs=VMEM,
        scratch_shapes=[pltpu.VMEM((width, tokens), F32)],
        compiler_params=pltpu.CompilerParams(vmem_limit_bytes=16 << 20),
    )(order, cotangent)


def pair(first, second, upper):
    first, second = first.astype(F32), second.astype(F32)
    even = jnp.where(upper, first, pltpu.roll(second, 4, 0))
    odd = jnp.where(upper, pltpu.roll(first, 4, 0), second)
    return even.astype(BF16), odd.astype(BF16)


def arrange_kernel(order_ref, *refs):
    *gathered, out_ref = refs
    tokens = order_ref.shape[0]
    row = 0
    while gathered:
        total, taken = 0, 0
        while taken < tokens:
            piece = gathered.pop(0)
            count = piece.shape[0]
            total = total + lax.dot_general(
                order_ref[taken : taken + count, :],
                piece[...],
                (((0,), (0,)), ((), ())),
                preferred_element_type=F32,
            )
            taken += count
        out_ref[row : row + tokens, :] = total.astype(BF16)
        row += tokens


def arrange(order, gathered):
    rows, width = sum(part.shape[0] for part in gathered), gathered[0].shape[1]
    return pl.pallas_call(
        arrange_kernel,
        out_shape=jax.ShapeDtypeStruct((rows, width), BF16),
        in_specs=[VMEM] * (1 + len(gathered)),
        out_specs=VMEM,
        compiler_params=pltpu.CompilerParams(vmem_limit_bytes=24 << 20),
        cost_estimate=pl.CostEstimate(
            flops=2 * rows * order.shape[0] * width,
            bytes_accessed=4 * rows * width,
            transcendentals=0,
        ),
    )(order, *gathered)


def weight_kernel(scale, spread_ref, inputs_ref, own_ref, other_ref, left):
    x = spread_ref.shape[1]
    half = spread_ref.shape[0] // 2
    tiles = half // 2
    x_here, c_here = lax.axis_index("x"), lax.axis_index("c")
    upper = lax.broadcasted_iota(jnp.int32, (8, LANES), 0) < 4
    for k in range(x):
        block = lax.rem(x_here - k + x, x)
        for part in range(2):
            core = c_here if part == 0 else 1 - c_here

            def place(i, carry, k=k, block=block, part=part, core=core):
                pairs = [
                    pair(
                        spread_ref[2 * (2 * i + n) + core, block],
                        spread_ref[half + 2 * (2 * i + n) + core, block],
                        upper,
                    )
                    for n in range(2)
                ]
                at = pl.multiple_of(part * tiles * 8 + i * 16, 16)
                for parity in range(2):
                    col = (2 * k + parity) * LANES
                    left[pl.ds(at, 16), col : col + LANES] = jnp.concatenate(
                        [pairs[0][parity], pairs[1][parity]], 0
                    )
                return carry

            lax.fori_loop(0, tiles // 2, place, 0, unroll=4)
    y = (jnp.dot(left[...], inputs_ref[...], preferred_element_type=F32) * scale).astype(BF16)
    own_ref[...] = y[: tiles * 8, :]
    other_ref[...] = y[tiles * 8 :, :]


def weight_part(spread, arranged, scale):
    count = spread.shape[0]
    depth, width = arranged.shape
    rows = count * 4
    return pl.pallas_call(
        functools.partial(weight_kernel, scale),
        out_shape=[jax.ShapeDtypeStruct((rows // 2, width), BF16)] * 2,
        in_specs=[VMEM, VMEM],
        out_specs=[VMEM, VMEM],
        scratch_shapes=[pltpu.VMEM((rows, depth), BF16)],
        compiler_params=pltpu.CompilerParams(vmem_limit_bytes=24 << 20),
        cost_estimate=pl.CostEstimate(
            flops=2 * rows * depth * width,
            bytes_accessed=4 * depth * width,
            transcendentals=0,
        ),
    )(spread, arranged)


def project_kernel(order_ref, weights_ref, *refs):
    *home, mine_ref, theirs_ref, columns, part, matrix, arrived = refs
    copy = pltpu.make_async_copy(weights_ref, matrix, arrived)
    copy.start()
    x = len(home)
    half = home[0].shape[0] // 2
    width = weights_ref.shape[0]
    yl = width // (LANES * x)
    x_here, sign = lax.axis_index("x"), lax.axis_index("s")
    upper = lax.broadcasted_iota(jnp.int32, (8, LANES), 0) < 4
    per = half // yl
    for k in range(x):
        block = lax.rem(x_here - k + x, x)
        for y in range(yl):

            def place(i, carry, k=k, y=y, block=block):
                q = y * per + 2 * i
                tile_pairs = [
                    pair(home[k][q + n], home[k][half + q + n], upper) for n in range(2)
                ]
                row = pl.multiple_of((y * x + block) * LANES + i * 16, 16)
                for parity in range(2):
                    columns[pl.ds(row, 16), parity * LANES : (parity + 1) * LANES] = (
                        jnp.concatenate([tile_pairs[0][parity], tile_pairs[1][parity]], 0)
                    )
                return carry

            lax.fori_loop(0, per // 2, place, 0, unroll=4)
    copy.wait()
    part[...] = lax.dot_general(
        columns[...], matrix[...], (((0,), (0,)), ((), ())), preferred_element_type=F32
    ).astype(BF16)
    whole = jnp.dot(order_ref[...], part[...], preferred_element_type=F32).astype(BF16)
    side = width // 2

    @pl.when(sign == 0)
    def _():
        mine_ref[...] = whole[:, :side]
        theirs_ref[...] = whole[:, side:]

    @pl.when(sign == 1)
    def _():
        mine_ref[...] = whole[:, side:]
        theirs_ref[...] = whole[:, :side]


def project(order, weights, home):
    tokens, width = order.shape[0], weights.shape[0]
    return pl.pallas_call(
        project_kernel,
        out_shape=[jax.ShapeDtypeStruct((tokens, width // 2), BF16)] * 2,
        in_specs=[VMEM, ANY] + [VMEM] * len(home),
        out_specs=[VMEM, VMEM],
        scratch_shapes=[
            pltpu.VMEM((width, tokens), BF16),
            pltpu.VMEM((tokens, width), BF16),
            pltpu.VMEM((width, width), BF16),
            pltpu.SemaphoreType.DMA,
        ],
        compiler_params=pltpu.CompilerParams(vmem_limit_bytes=24 << 20),
        cost_estimate=pl.CostEstimate(
            flops=2 * tokens * width * width, bytes_accessed=4 * width * width, transcendentals=0
        ),
    )(order, weights, *home)


def body(inputs, cotangent, weights, filter_taps):
    sizes = SIZES
    s, yl, x, z, c = sizes
    tokens, width = inputs.shape
    half = tokens // 2
    groups = yl * x * z * c
    x_here = lax.axis_index("x")
    row = lax.broadcasted_iota(jnp.int32, (tokens, tokens), 0)
    col = lax.broadcasted_iota(jnp.int32, (tokens, tokens), 1)
    order = (row == 2 * (col % half) + col // half).astype(BF16)

    send = turn(order, cotangent)
    signal = lax.all_to_all(send, ("yl", "x", "z", "c"), split_axis=0, concat_axis=0, tiled=True)

    taps = toeplitz(filter_taps)
    taps, inputs = lax.optimization_barrier((taps, inputs))
    before, after = along(inputs, "x", x, 1), along(inputs, "x", x, x - 1)

    result = filtered(signal, taps, sizes).reshape(s * yl * z * c, x, 8, half)
    result, before, after = lax.optimization_barrier((result, before, after))
    gathered = [
        inputs,
        before,
        along(before[:half], "x", x, 1),
        along(after[half:], "x", x, x - 1),
        after,
    ]
    spread = lax.all_to_all(result, ("s", "yl", "z", "c"), split_axis=0, concat_axis=0, tiled=True)
    home = [
        lax.dynamic_index_in_dim(spread, lax.rem(x_here + k, x), 1, keepdims=False)
        for k in range(x)
    ]

    grad_scale = 1.0 / math.sqrt(tokens * groups)
    own, other = weight_part(spread, arrange(order, gathered), grad_scale)
    other, *home = lax.optimization_barrier((other, *home))
    home = [home[0]] + [along(home[k], "x", x, k) for k in range(1, x)]
    other = along(other, "c", c, 1)
    reduced = (own.astype(F32) + other.astype(F32)).astype(BF16).reshape(yl * z, 8, width)
    _, *home = lax.optimization_barrier((reduced, *home))
    mine, theirs = project(order, weights[0], home)
    arrived = jnp.concatenate([along(theirs[:half], "s", s, 1), along(theirs[half:], "s", s, 1)])
    pieces = lax.all_to_all(reduced, ("yl", "z"), split_axis=0, concat_axis=0, tiled=True)
    weight_grad = jnp.sum(pieces.astype(F32), 0)
    input_grad = (mine.astype(F32) + arrived.astype(F32)).astype(BF16)
    return input_grad, weight_grad[None]


def solution(mesh):
    fine = Mesh(mesh.devices.reshape(SIZES), AXES)
    context = ("yl", "x", "z", "c")
    in_specs = (P(context, None), P(context, None), P("s", None, None), P())
    out_specs = (P(context, "s"), P("s", context, None))
    return jax.shard_map(body, mesh=fine, in_specs=in_specs, out_specs=out_specs, check_vma=False)
```
